128 devices in a mesh: lat: 4 (over x), lon: 32 (over z, y, core).
Axes of the slice: x: 4, y: 4, z: 4, core: 2. Of those that a mesh axis runs over, the one named last changes fastest.
Arguments:
- lattice_feature_values: bfloat16 [131072, 227], P(('lat', 'lon')), may hold values from -6 to 6
- cotangent: bfloat16 [131072, 227], P(('lat', 'lon')), may hold values from -0.0390625 to 0.0390625
- embed_weight: bfloat16 [227, 512], replicated, may hold values from -0.375 to 0.375
- encode_weight: bfloat16 [512, 512], replicated, may hold values from -0.09375 to 0.09375
- sender_weight: bfloat16 [2, 512, 512], replicated, may hold values from -0.25 to 0.25
- receiver_weight: bfloat16 [2, 512, 512], replicated, may hold values from -0.25 to 0.25
- update_weight: bfloat16 [2, 512, 512], replicated, may hold values from -0.09375 to 0.09375
- decode_weight: bfloat16 [512, 227], replicated, may hold values from -0.25 to 0.25
- encode_lists: int32 [512, 64], P(('lat', 'lon')), may hold values from 0 to 1023, as said below
- encode_sources: int32 [32768, 8], P(('lat', 'lon')), may hold values from 0 to 1279, as said below
- mesh_lists: int32 [16384, 4], P(('lat', 'lon')), may hold values from 0 to 255, as said below
- mesh_sources: int32 [32768, 8], P(('lat', 'lon')), may hold values from 0 to 767, as said below
- decode_lists: int32 [512, 64], P(('lat', 'lon')), may hold values from 0 to 255, as said below
- decoder_edge_sources: int32 [131072, 3], P(('lat', 'lon')), may hold values from 0 to 511, as said below
Outputs:
- prediction_field: bfloat16 [131072, 227], P(('lat', 'lon'))
- embed_matrix_slope: float32 [227, 512], P(None, ('lat', 'lon'))
- encode_matrix_slope: float32 [512, 512], P(None, ('lat', 'lon'))
- source_matrix_slope: float32 [2, 512, 512], P(None, None, ('lat', 'lon'))
- target_matrix_slope: float32 [2, 512, 512], P(None, None, ('lat', 'lon'))
- refresh_matrix_slope: float32 [2, 512, 512], P(None, None, ('lat', 'lon'))
- decode_matrix_slope: float32 [512, 227], P(('lat', 'lon'))
The draws below stay inside these ranges and needn't reach their ends.
Inputs may be any that keep to these rules, and one draw needn't show every extreme that they name: `encode_lists`: row p * 4 + k names rows of device p's own grid points listed for its neighbour in direction k. `encode_sources`: each mesh node has exactly 8 entries, read as in the first step. Every slot that an existing neighbour lists for a device is read by it; no entry names a neighbour beyond the first or last band. `mesh_lists`: row p * 128 + d names rows of device p's own mesh nodes that device d may read. `mesh_sources`: each mesh node has exactly 8 entries. Of the list that device p keeps for device d, d reads a prefix: all 4 slots when p lies beside d in its band or on its sector, or when d lies in one band that the draw chooses, else 1 to 2 slots; every slot of a prefix is read, no slot past it. `decode_lists`: row p * 4 + k names rows of device p's own mesh nodes listed for its neighbour in direction k. `decoder_edge_sources`: each grid point has exactly 3 entries; neighbour slots are read as for encode_sources.
All inputs are finite; a program needn't handle non-finite values.
Results may differ from the reference program's by a relative error of at most 0.015.
Values may be sent and summed in bfloat16 or wider, within the bound.
A program may use at most 128 MiB of HBM per device.

```python
import jax
import jax.numpy as jnp

LATENT = 512
CHANNELS = 227
GRID_ROWS = 1024
MESH_ROWS = 256
LAYERS = 2
ENCODE_DEGREE = 8
MESH_DEGREE = 8
DECODE_DEGREE = 3
SLOTS = 4
HALO = 64
BANDS = 4
SECTORS = 32
PEERS = 128
GRID_ALL = 131072
MESH_ALL = 32768


def link_tables(key, sending_rows, receiving_rows, degree):
    key_dense, key_count, key_lists, key_local, key_order = jax.random.split(key, 5)
    device_ids = jnp.arange(PEERS, dtype=jnp.int32)
    band_index = device_ids // SECTORS
    sector_index = device_ids % SECTORS
    dense_band = jax.random.randint(key_dense, (), 0, BANDS)
    same_band = band_index[:, None] == band_index[None, :]
    same_sector = sector_index[:, None] == sector_index[None, :]
    cycle_gap = (sector_index[:, None] - sector_index[None, :]) % SECTORS
    band_gap = jnp.abs(band_index[:, None] - band_index[None, :])
    beside = same_band & ((cycle_gap == 1) | (cycle_gap == SECTORS - 1)) | same_sector & (band_gap == 1)
    full = beside | (band_index[None, :] == dense_band)
    partial_value = jax.random.randint(key_count, (PEERS, PEERS), 1, SLOTS // 2 + 1)
    counts = jnp.where(full, SLOTS, partial_value)
    lists = jax.random.randint(key_lists, (PEERS * PEERS, SLOTS), 0, sending_rows)
    edges = receiving_rows * degree
    position = jnp.arange(edges, dtype=jnp.int32)
    slot_peer = jnp.minimum(position // SLOTS, PEERS - 1)
    slot_place = position % SLOTS
    readable = (position < PEERS * SLOTS)[None, :] & (slot_place[None, :] < counts[slot_peer, :].T)
    local_pick = jax.random.randint(key_local, (PEERS, edges), 0, sending_rows)
    values = jnp.where(readable, sending_rows + position[None, :], local_pick)
    order_keys = jax.random.split(key_order, PEERS)
    orders = jax.vmap(lambda single: jax.random.permutation(single, edges))(order_keys)
    values = jnp.take_along_axis(values, orders, axis=1)
    return (lists.astype(jnp.int32), values.reshape(PEERS * receiving_rows, degree).astype(jnp.int32))


def near_tables(key, sending_rows, receiving_rows, degree):
    key_lists, key_local, key_order = jax.random.split(key, 3)
    device_ids = jnp.arange(PEERS, dtype=jnp.int32)
    band_index = (device_ids // SECTORS)[:, None]
    edges = receiving_rows * degree
    position = jnp.arange(edges, dtype=jnp.int32)[None, :]
    facing = jnp.minimum(position // HALO, 3)
    exists = jnp.where(facing == 2, band_index > 0, jnp.where(facing == 3, band_index < BANDS - 1, True))
    readable = (position < 4 * HALO) & exists
    local_pick = jax.random.randint(key_local, (PEERS, edges), 0, sending_rows)
    values = jnp.where(readable, sending_rows + position, local_pick)
    order_keys = jax.random.split(key_order, PEERS)
    orders = jax.vmap(lambda single: jax.random.permutation(single, edges))(order_keys)
    values = jnp.take_along_axis(values, orders, axis=1)
    lists = jax.random.randint(key_lists, (PEERS * 4, HALO), 0, sending_rows)
    return (lists.astype(jnp.int32), values.reshape(PEERS * receiving_rows, degree).astype(jnp.int32))


def draw_encode_lists(key, part):
    return near_tables(jax.random.fold_in(key, 11), GRID_ROWS, MESH_ROWS, ENCODE_DEGREE)[0]


def draw_encode_sources(key, part):
    return near_tables(jax.random.fold_in(key, 11), GRID_ROWS, MESH_ROWS, ENCODE_DEGREE)[1]


def draw_mesh_lists(key, part):
    return link_tables(jax.random.fold_in(key, 22), MESH_ROWS, MESH_ROWS, MESH_DEGREE)[0]


def draw_mesh_sources(key, part):
    return link_tables(jax.random.fold_in(key, 22), MESH_ROWS, MESH_ROWS, MESH_DEGREE)[1]


def draw_decode_lists(key, part):
    return near_tables(jax.random.fold_in(key, 33), MESH_ROWS, GRID_ROWS, DECODE_DEGREE)[0]


def draw_decoder_edge_sources(key, part):
    return near_tables(jax.random.fold_in(key, 33), MESH_ROWS, GRID_ROWS, DECODE_DEGREE)[1]


def steps_of(own_key, extent, pieces, low, largest):
    gain = 1.0
    for dim, shards_of in pieces:
        steps = jax.random.uniform(jax.random.fold_in(jax.random.fold_in(own_key, 6), dim), (shards_of,), jnp.float32, low / len(pieces), largest / len(pieces))
        gain = gain * jnp.repeat(jnp.exp(steps), extent[dim] // shards_of).reshape((-1,) + (1,) * (len(extent) - 1 - dim))
    return gain


def centred(key, dims, scale, most, pieces=(), kind=jnp.bfloat16):
    level = steps_of(key, dims, pieces, -0.22, 0.18) if pieces else 1.0
    values = jax.random.normal(key, dims, jnp.float32) * scale * level
    return jnp.minimum(jnp.maximum(values, -most), most).astype(kind)


def setup_inputs(seed: int = 0) -> dict:
    streams_of = jax.random.split(jax.random.key(seed), 15)
    return {
        "lattice_feature_values": centred(streams_of[0], (GRID_ALL, CHANNELS), 1.0, 6.0, ((0, 128),)),
        "cotangent": centred(streams_of[1], (GRID_ALL, CHANNELS), (1.0 / GRID_ALL ** 0.5), 0.0390625, ((0, 128),)),
        "embed_weight": centred(streams_of[2], (CHANNELS, LATENT), CHANNELS ** -0.5, 0.375),
        "encode_weight": centred(streams_of[3], (LATENT, LATENT), (LATENT * ENCODE_DEGREE) ** -0.5, 0.09375),
        "sender_weight": centred(streams_of[4], (LAYERS, LATENT, LATENT), LATENT ** -0.5, 0.25),
        "receiver_weight": centred(streams_of[5], (LAYERS, LATENT, LATENT), LATENT ** -0.5, 0.25),
        "update_weight": centred(streams_of[6], (LAYERS, LATENT, LATENT), (LATENT * MESH_DEGREE) ** -0.5, 0.09375),
        "decode_weight": centred(streams_of[7], (LATENT, CHANNELS), LATENT ** -0.5, 0.25),
        "encode_lists": draw_encode_lists(jax.random.fold_in(streams_of[14], 71), 0),
        "encode_sources": draw_encode_sources(jax.random.fold_in(streams_of[14], 71), 0),
        "mesh_lists": draw_mesh_lists(jax.random.fold_in(streams_of[14], 71), 0),
        "mesh_sources": draw_mesh_sources(jax.random.fold_in(streams_of[14], 71), 0),
        "decode_lists": draw_decode_lists(jax.random.fold_in(streams_of[14], 71), 0),
        "decoder_edge_sources": draw_decoder_edge_sources(jax.random.fold_in(streams_of[14], 71), 0),
    }


def silu_slope(inner):
    sigma = jax.nn.sigmoid(inner)
    return sigma * (1.0 + inner * (1.0 - sigma))


def resolve(lists, sources, sending_rows):
    total = sources.shape[0]
    receiving = total // PEERS
    owner = (jnp.arange(total, dtype=jnp.int32) // receiving)[:, None]
    offset = jnp.maximum(sources - sending_rows, 0)
    sender = offset // SLOTS
    place = offset % SLOTS
    listed = lists[sender * PEERS + owner, place]
    local_row = owner * sending_rows + sources
    remote_row = sender * sending_rows + listed
    return jnp.where(sources < sending_rows, local_row, remote_row).astype(jnp.int32)


def resolve_near(lists, sources, sending_rows):
    total = sources.shape[0]
    receiving = total // PEERS
    owner = (jnp.arange(total, dtype=jnp.int32) // receiving)[:, None]
    owner_band = owner // SECTORS
    owner_sector = owner % SECTORS
    offset = jnp.maximum(sources - sending_rows, 0)
    facing = offset // HALO
    place = offset % HALO
    band_step = jnp.where(facing == 2, -1, jnp.where(facing == 3, 1, 0))
    sector_step = jnp.where(facing == 0, -1, jnp.where(facing == 1, 1, 0))
    near_band = jnp.clip(owner_band + band_step, 0, BANDS - 1)
    near_sector = (owner_sector + sector_step + SECTORS) % SECTORS
    neighbour = (near_band * SECTORS + near_sector).astype(jnp.int32)
    opposite = facing + 1 - 2 * (facing % 2)
    listed = lists[neighbour * 4 + opposite, place]
    local_row = owner * sending_rows + sources
    remote_row = neighbour * sending_rows + listed
    return jnp.where(sources < sending_rows, local_row, remote_row).astype(jnp.int32)


def collected_grand_accumulation(table, rows):
    result = jnp.zeros((rows.shape[0], table.shape[1]), jnp.float32)
    for column in range(rows.shape[1]):
        result = result + table[rows[:, column]].astype(jnp.float32)
    return result


def spread(grads, rows, total):
    result = jnp.zeros((total, grads.shape[1]), jnp.float32)
    for column in range(rows.shape[1]):
        result = result.at[rows[:, column]].add(grads)
    return result


def reference(lattice_feature_values, cotangent, embed_weight, encode_weight, sender_weight, receiver_weight, update_weight, decode_weight, encode_lists, encode_sources, mesh_lists, mesh_sources, decode_lists, decoder_edge_sources):
    encode_rows = resolve_near(encode_lists, encode_sources, GRID_ROWS)
    mesh_rows = resolve(mesh_lists, mesh_sources, MESH_ROWS)
    decode_result_lines = resolve_near(decode_lists, decoder_edge_sources, MESH_ROWS)
    embed_inner = jnp.dot(lattice_feature_values, embed_weight, preferred_element_type=jnp.float32)
    grid_latent = jax.nn.silu(embed_inner).astype(jnp.bfloat16)
    encode_input = collected_grand_accumulation(grid_latent, encode_rows).astype(jnp.bfloat16)
    encode_inner = jnp.dot(encode_input, encode_weight, preferred_element_type=jnp.float32)
    mesh_latent = jax.nn.silu(encode_inner).astype(jnp.bfloat16)
    saved = []
    for layer in range(LAYERS):
        sender_rows = jnp.dot(mesh_latent, sender_weight[layer], preferred_element_type=jnp.float32).astype(jnp.bfloat16)
        receiver_rows = jnp.dot(mesh_latent, receiver_weight[layer], preferred_element_type=jnp.float32)
        aggregate = jnp.zeros(receiver_rows.shape, jnp.float32)
        for column in range(MESH_DEGREE):
            aggregate = aggregate + jax.nn.silu(sender_rows[mesh_rows[:, column]].astype(jnp.float32) + receiver_rows)
        aggregate = aggregate.astype(jnp.bfloat16)
        saved.append((mesh_latent, sender_rows, receiver_rows, aggregate))
        update = jnp.dot(aggregate, update_weight[layer], preferred_element_type=jnp.float32)
        mesh_latent = (mesh_latent.astype(jnp.float32) + update).astype(jnp.bfloat16)
    decode_mapped_values = jnp.dot(mesh_latent, decode_weight, preferred_element_type=jnp.float32).astype(jnp.bfloat16)
    prediction_field = (lattice_feature_values.astype(jnp.float32) + collected_grand_accumulation(decode_mapped_values, decode_result_lines)).astype(jnp.bfloat16)

    decode_back = spread(cotangent.astype(jnp.float32), decode_result_lines, MESH_ALL).astype(jnp.bfloat16)
    decode_matrix_slope = jnp.dot(mesh_latent.T, decode_back, preferred_element_type=jnp.float32)
    latent_back = jnp.dot(decode_back, decode_weight.T, preferred_element_type=jnp.float32)
    sender_list, receiver_list, update_list = [], [], []
    for layer in reversed(range(LAYERS)):
        old_latent, sender_rows, receiver_rows, aggregate = saved[layer]
        out_back = latent_back.astype(jnp.bfloat16)
        update_list.append(jnp.dot(aggregate.T, out_back, preferred_element_type=jnp.float32))
        aggregate_back = jnp.dot(out_back, update_weight[layer].T, preferred_element_type=jnp.float32)
        receiver_back = jnp.zeros(receiver_rows.shape, jnp.float32)
        sender_back = jnp.zeros(receiver_rows.shape, jnp.float32)
        for column in range(MESH_DEGREE):
            inner = sender_rows[mesh_rows[:, column]].astype(jnp.float32) + receiver_rows
            inner_back = aggregate_back * silu_slope(inner)
            receiver_back = receiver_back + inner_back
            sender_back = sender_back.at[mesh_rows[:, column]].add(inner_back)
        sender_b = sender_back.astype(jnp.bfloat16)
        receiver_b = receiver_back.astype(jnp.bfloat16)
        sender_list.append(jnp.dot(old_latent.T, sender_b, preferred_element_type=jnp.float32))
        receiver_list.append(jnp.dot(old_latent.T, receiver_b, preferred_element_type=jnp.float32))
        latent_back = latent_back + jnp.dot(sender_b, sender_weight[layer].T, preferred_element_type=jnp.float32)
        latent_back = latent_back + jnp.dot(receiver_b, receiver_weight[layer].T, preferred_element_type=jnp.float32)
    encode_back = (latent_back * silu_slope(encode_inner)).astype(jnp.bfloat16)
    encode_matrix_slope = jnp.dot(encode_input.T, encode_back, preferred_element_type=jnp.float32)
    input_back = jnp.dot(encode_back, encode_weight.T, preferred_element_type=jnp.float32)
    grid_back = spread(input_back, encode_rows, GRID_ALL)
    embed_back = (grid_back * silu_slope(embed_inner)).astype(jnp.bfloat16)
    embed_matrix_slope = jnp.dot(lattice_feature_values.T, embed_back, preferred_element_type=jnp.float32)
    source_matrix_slope = jnp.stack(sender_list[::-1])
    target_matrix_slope = jnp.stack(receiver_list[::-1])
    refresh_matrix_slope = jnp.stack(update_list[::-1])
    return (prediction_field, embed_matrix_slope, encode_matrix_slope, source_matrix_slope, target_matrix_slope, refresh_matrix_slope, decode_matrix_slope)
```

```python
import functools

import jax
import jax.numpy as jnp
from jax import lax
from jax.experimental import pallas as pl
from jax.experimental.pallas import tpu as pltpu
from jax.sharding import PartitionSpec as P

BF = jnp.bfloat16
F32 = jnp.float32
MESH = pl.DeviceIdType.MESH

BANDS, SECTORS, PEERS = 4, 32, 128
LATENT, CHANNELS, PADDED = 512, 227, 256
GRID, NODES, HALO, SLOTS, DEGREE = 1024, 256, 64, 4, 8
EDGES = NODES * DEGREE
FAR = PEERS * SLOTS


def mm(a, b):
    return lax.dot_general(a, b, (((1,), (0,)), ((), ())), preferred_element_type=F32)


def mmt(a, b):
    return lax.dot_general(a, b, (((1,), (1,)), ((), ())), preferred_element_type=F32)


def tmm(a, b):
    return lax.dot_general(a, b, (((0,), (0,)), ((), ())), preferred_element_type=F32)


def sigmoid(v):
    return 0.5 * jnp.tanh(0.5 * v) + 0.5


def iota(shape, dim):
    return lax.broadcasted_iota(jnp.int32, shape, dim)


def hot(mask):
    return jnp.where(mask, 1.0, 0.0).astype(BF)


def column(row):
    return jnp.transpose(jnp.broadcast_to(row, (8, row.shape[1])))[:, :1]


class Refs:
    def __init__(self, named):
        for name, ref in named.items():
            if isinstance(ref, list):
                ref = [Refs(each) for each in ref]
            setattr(self, name, ref)


GROUPS = (1024, 1536, 1024, 512)


def scratch():
    vm = pltpu.VMEM
    sems = pltpu.SemaphoreType.DMA
    return dict(
        xp=vm((PADDED, GRID), BF),
        cp=vm((PADDED, GRID), BF),
        wep=vm((PADDED, LATENT), BF),
        dwp=vm((PADDED, LATENT), BF),
        grid_ext=vm((GRID + 4 * HALO, LATENT), BF),
        gslope=vm((GRID, LATENT), BF),
        enc_c=vm((NODES, GRID + 4 * HALO), BF),
        enc_t=vm((GRID + 4 * HALO, NODES), BF),
        dec_t=vm((NODES + 4 * HALO, GRID), BF),
        oh_loc=vm((EDGES, NODES), BF),
        oh_far=vm((EDGES, FAR), BF),
        t_loc=vm((NODES, EDGES), BF),
        t_far=vm((FAR, EDGES), BF),
        list_r=vm((FAR, NODES), BF),
        list_t=vm((NODES, FAR), BF),
        p_own=vm((NODES, LATENT), BF),
        p_oth=vm((NODES, LATENT), BF),
        enc_in=vm((NODES, LATENT), BF),
        enc_slope=vm((NODES, LATENT), F32),
        mesh=vm((3, NODES, LATENT), BF),
        agg=vm((2, NODES, LATENT), BF),
        base=vm((EDGES, LATENT), F32),
        slope=vm((EDGES, LATENT), BF),
        ib=vm((EDGES, LATENT), BF),
        rb=vm((NODES, LATENT), BF),
        ab=vm((NODES, LATENT), F32),
        ob=vm((NODES, LATENT), BF),
        lat=vm((NODES, LATENT), F32),
        dback=vm((NODES, PADDED), BF),
        dext=vm((NODES, PADDED), F32),
        sback=vm((NODES, LATENT), F32),
        gback=vm((GRID, LATENT), F32),
        eb=vm((GRID, LATENT), BF),
        far=vm((FAR, LATENT), BF),
        packed=vm((4 * FAR, 128), F32),
        ns0=vm((4 * HALO, LATENT), BF),
        ns1=vm((4 * HALO, PADDED), BF),
        nr1=vm((4 * HALO, PADDED), BF),
        ns2=vm((4 * HALO, LATENT), BF),
        mesh_ext=vm((NODES + 4 * HALO, LATENT), BF),
        ns3=vm((4 * HALO, LATENT), BF),
        nr3=vm((4 * HALO, LATENT), BF),
        near_sem=sems((4, 2)),
        far_sem=sems((4, 2)),
        fars=[dict(source=vm((4 * FAR, 128), BF), target=vm((4 * FAR, 128), BF)) for _ in range(4)],
        groups=[
            dict(
                own=vm((NODES, width), F32),
                sc=vm((NODES, width), BF),
                rc=vm((NODES, width), BF),
                sx=vm((NODES, width), BF),
                rx=vm((192, width), BF),
                fp=vm((width // 2, 128), F32),
                sp=vm((width // 2, 128), BF),
                rp=vm((width // 2, 128), BF),
                sem=sems((3, 2)),
            )
            for width in GROUPS
        ],
    )


def kernel(tree, xt, ct, we, wn, ws, wr, wu, dwt, el, es, ml, ms, dl, ds_, *rest):
    out_pred, out_embed, out_encode, out_source, out_target, out_refresh, out_decode = rest[:7]
    r = Refs(jax.tree.unflatten(tree, rest[7:]))
    ga, gb, gc, gd = r.groups
    b = lax.axis_index("lat")
    c = lax.axis_index("lon")
    me = b * SECTORS + c
    core = lax.rem(c, 2)
    place = c // 2

    barrier = pltpu.get_barrier_semaphore()

    def greet(t, carry):
        u = lax.rem(b + t // SECTORS, BANDS)
        v = lax.rem(c + lax.rem(t, SECTORS), SECTORS)
        pl.semaphore_signal(barrier, inc=1, device_id=(u, v), device_id_type=MESH)
        return carry

    lax.fori_loop(1, PEERS, greet, 0)

    neighbours = (
        (b, lax.rem(c + SECTORS - 1, SECTORS)),
        (b, lax.rem(c + 1, SECTORS)),
        (lax.rem(b + BANDS - 1, BANDS), c),
        (lax.rem(b + 1, BANDS), c),
    )

    def drain(ref, sem):
        pltpu.make_async_copy(ref, ref, sem).wait()

    def near_start(i, source, target):
        for k in range(4):
            pltpu.make_async_remote_copy(
                source.at[pl.ds(k * HALO, HALO)],
                target.at[pl.ds((k ^ 1) * HALO, HALO)],
                r.near_sem.at[i, 0],
                r.near_sem.at[i, 1],
                device_id=neighbours[k],
                device_id_type=MESH,
            ).start()

    def near_wait(i, source, target):
        drain(target, r.near_sem.at[i, 1])
        drain(source, r.near_sem.at[i, 0])

    def far_start(i):
        source, target = r.fars[i].source, r.fars[i].target
        mine = pl.ds(pl.multiple_of(me * 16, 16), 16)

        def send(t, carry):
            u = lax.rem(b + lax.rem(t, BANDS), BANDS)
            v = lax.rem(c + t // BANDS, SECTORS)
            block = pl.ds(pl.multiple_of((u * SECTORS + v) * 16, 16), 16)
            pltpu.make_async_remote_copy(
                source.at[block],
                target.at[mine],
                r.far_sem.at[i, 0],
                r.far_sem.at[i, 1],
                device_id=(u, v),
                device_id_type=MESH,
            ).start()
            return carry

        lax.fori_loop(1, PEERS, send, 0)
        target[mine, :] = source[mine, :]

    def far_wait(i):
        rest_of = pl.ds(0, 16 * (PEERS - 1))
        drain(r.fars[i].target.at[rest_of], r.far_sem.at[i, 1])
        drain(r.fars[i].source.at[rest_of], r.far_sem.at[i, 0])

    packed = r.packed

    def pack(value, target):
        for i in range(SLOTS):
            for j in range(4):
                packed[pl.ds(4 * j + i, PEERS, stride=16), :] = value[
                    i * PEERS : (i + 1) * PEERS, j * 128 : (j + 1) * 128
                ]
        target[...] = packed[...].astype(BF)

    def unpack(source):
        packed[...] = source[...].astype(F32)
        for i in range(SLOTS):
            for j in range(4):
                r.far[i * PEERS : (i + 1) * PEERS, j * 128 : (j + 1) * 128] = packed[
                    pl.ds(4 * j + i, PEERS, stride=16), :
                ].astype(BF)

    def turned(value):
        return (
            mmt(r.p_own[...], value).astype(BF),
            mmt(r.p_oth[...], value).astype(BF),
        )

    def gradient(g, at, width, sides, right, product=mm):
        g.own[:, at : at + width] = product(sides[0], right)
        g.sc[:, at : at + width] = product(sides[1], right).astype(BF)

    def core_start(g):
        pltpu.make_async_remote_copy(
            g.sc,
            g.rc,
            g.sem.at[0, 0],
            g.sem.at[0, 1],
            device_id=(b, c + 1 - 2 * core),
            device_id_type=MESH,
        ).start()

    def core_wait(g):
        drain(g.rc, g.sem.at[0, 1])
        drain(g.sc, g.sem.at[0, 0])
        own, got, out = g.own, g.rc, g.sx
        total = own[...] + got[...].astype(F32)
        own[...] = total
        out[...] = total.astype(BF)

    def band_start(g):
        for t in range(1, BANDS):
            u = lax.rem(b + t, BANDS)
            pltpu.make_async_remote_copy(
                g.sx.at[pl.ds(pl.multiple_of(u * 64, 64), 64)],
                g.rx.at[pl.ds((t - 1) * 64, 64)],
                g.sem.at[1, 0],
                g.sem.at[1, 1],
                device_id=(u, c),
                device_id_type=MESH,
            ).start()

    def band_wait(g):
        drain(g.rx, g.sem.at[1, 1])
        drain(g.sx.at[pl.ds(0, 192)], g.sem.at[1, 0])
        width = g.sc.shape[1]
        rows = width // 32
        got, flat = g.rx, g.fp
        mine = pl.ds(pl.multiple_of(b * 64, 64), 64)
        total = g.own[mine, :]
        for t in range(3):
            total = total + got[t * 64 : (t + 1) * 64, :].astype(F32)
        for j in range(width // 128):
            for i in range(4):
                flat[pl.ds(4 * j + i, 16, stride=rows), :] = total[
                    i * 16 : (i + 1) * 16, j * 128 : (j + 1) * 128
                ]
        g.sp[...] = flat[...].astype(BF)

    def plane_start(g):
        rows = g.sc.shape[1] // 32
        source, target = g.sp, g.rp
        mine = pl.ds(pl.multiple_of(place * rows, 16), rows)

        def send(t, carry):
            q = lax.rem(place + t, 16)
            pltpu.make_async_remote_copy(
                source.at[pl.ds(pl.multiple_of(q * rows, 16), rows)],
                target.at[mine],
                g.sem.at[2, 0],
                g.sem.at[2, 1],
                device_id=(b, q * 2 + core),
                device_id_type=MESH,
            ).start()
            return carry

        lax.fori_loop(1, 16, send, 0)
        target[mine, :] = source[mine, :]

    def plane_wait(g):
        rows = g.sc.shape[1] // 32
        rest_of = pl.ds(0, 15 * rows)
        drain(g.rp.at[rest_of], g.sem.at[2, 1])
        drain(g.sp.at[rest_of], g.sem.at[2, 0])
        got = g.rp
        total = got[0:rows, :].astype(F32)
        for q in range(1, 16):
            total = total + got[q * rows : (q + 1) * rows, :].astype(F32)
        return total

    def deliver(total, at, write):
        for j in range(4):
            row = 4 * (at // 128 + j)
            write(j, total[row : row + 4, :])

    for target, source in ((r.xp, xt), (r.cp, ct), (r.wep, we), (r.dwp, dwt)):
        target[224:256, :] = jnp.zeros((32, source.shape[1]), BF)
        target[0:CHANNELS, :] = source[...]

    def embed(i, carry):
        rows = pl.ds(pl.multiple_of(i * 256, 256), 256)
        inner = tmm(r.xp[:, rows], r.wep[...])
        s = sigmoid(inner)
        value = inner * s
        r.grid_ext[rows, :] = value.astype(BF)
        r.gslope[rows, :] = (s + value * (1.0 - s)).astype(BF)
        return carry

    lax.fori_loop(0, 4, embed, 0)

    def near_row(lists):
        return jnp.concatenate([lists[k : k + 1, :] for k in range(4)], axis=1)

    encode_row = near_row(el)
    decode_row = near_row(dl)
    encode_pick = hot(column(encode_row) == iota((4 * HALO, GRID), 1))
    r.ns0[...] = mm(encode_pick, r.grid_ext[0:GRID, :]).astype(BF)

    pl.semaphore_wait(barrier, PEERS - 1)
    halo_grid = r.grid_ext.at[pl.ds(GRID, 4 * HALO)]
    near_start(0, r.ns0, halo_grid)

    for part in range(2):
        where = iota((NODES, GRID), 0) + part * NODES
        total = jnp.zeros((NODES, GRID), F32)
        for k in range(3):
            total = total + jnp.where(ds_[k : k + 1, :] == where, 1.0, 0.0)
        r.dec_t[part * NODES : (part + 1) * NODES, :] = total.astype(BF)
    r.ns1[...] = mmt(r.dec_t[NODES:, :], r.cp[...]).astype(BF)
    near_start(1, r.ns1, r.nr1)
    r.dext[...] = mmt(r.dec_t[0:NODES, :], r.cp[...])

    es_col = jnp.transpose(es[...])
    for part in range(5):
        where = iota((NODES, 256), 1) + part * 256
        where_t = iota((256, NODES), 0) + part * 256
        total = jnp.zeros((NODES, 256), F32)
        total_t = jnp.zeros((256, NODES), F32)
        for k in range(DEGREE):
            total = total + jnp.where(es_col[:, k : k + 1] == where, 1.0, 0.0)
            total_t = total_t + jnp.where(es[k : k + 1, :] == where_t, 1.0, 0.0)
        r.enc_c[:, part * 256 : (part + 1) * 256] = total.astype(BF)
        r.enc_t[part * 256 : (part + 1) * 256, :] = total_t.astype(BF)
    encode_local = mm(r.enc_c[:, 0:GRID], r.grid_ext[0:GRID, :])

    for i in range(SLOTS):
        row = ml[i : i + 1, :]
        r.list_r[i * PEERS : (i + 1) * PEERS, :] = hot(column(row) == iota((PEERS, NODES), 1))
        r.list_t[:, i * PEERS : (i + 1) * PEERS] = hot(row == iota((NODES, PEERS), 0))

    near_wait(0, r.ns0, halo_grid)
    encode_input = (encode_local + mm(r.enc_c[:, GRID:], r.grid_ext[GRID:, :])).astype(BF)
    r.enc_in[...] = encode_input
    encode_inner = mm(encode_input, wn[...])
    s = sigmoid(encode_inner)
    value = encode_inner * s
    r.mesh[0] = value.astype(BF)
    r.enc_slope[...] = s + value * (1.0 - s)

    def send_rows(layer):
        sender = mm(r.mesh[layer], ws[layer]).astype(BF)
        pack(mm(r.list_r[...], sender), r.fars[layer].source)
        far_start(layer)
        return sender

    def local_rows(layer, sender):
        receiver = mm(r.mesh[layer], wr[layer])
        for k in range(DEGREE):
            rows = slice(k * NODES, (k + 1) * NODES)
            r.base[rows, :] = mm(r.oh_loc[rows, :], sender) + receiver

    def far_rows(layer):
        far_wait(layer)
        unpack(r.fars[layer].target)

        def add(k, carry):
            rows = pl.ds(pl.multiple_of(k * NODES, NODES), NODES)
            r.base[rows, :] += mm(r.oh_far[rows, :], r.far[...])
            return carry

        lax.fori_loop(0, DEGREE, add, 0)

    sender = send_rows(0)

    def far_index(v):
        k = v - NODES
        return jnp.where(k >= 0, (k & 3) * PEERS + (k >> 2), -1)

    ms_row = ms[...]
    ms_col = jnp.transpose(ms_row)
    far_row = far_index(ms_row)
    far_col = far_index(ms_col)
    for k in range(DEGREE):
        rows = slice(k * NODES, (k + 1) * NODES)
        r.oh_loc[rows, :] = hot(ms_col[:, k : k + 1] == iota((NODES, NODES), 1))
        r.oh_far[rows, :] = hot(far_col[:, k : k + 1] == iota((NODES, FAR), 1))
        r.t_loc[:, rows] = hot(ms_row[k : k + 1, :] == iota((NODES, NODES), 0))
        r.t_far[:, rows] = hot(far_row[k : k + 1, :] == iota((FAR, NODES), 0))
    local_rows(0, sender)

    index = iota((NODES, LATENT), 0)
    first = (index // 64) * 128 + (index % 16) * 8 + (index // 16) % 4
    r.p_own[...] = hot(first + core * 4 == iota((NODES, LATENT), 1))
    r.p_oth[...] = hot(first + (1 - core) * 4 == iota((NODES, LATENT), 1))

    decode_spread = hot(decode_row == iota((NODES, 4 * HALO), 0))
    near_wait(1, r.ns1, r.nr1)
    decode_back = (r.dext[...] + mm(decode_spread, r.nr1[...])).astype(BF)
    r.dback[...] = decode_back
    latent_back = mm(decode_back, r.dwp[...])
    r.lat[...] = latent_back
    out_back = latent_back.astype(BF)
    r.ob[...] = out_back
    r.ab[...] = mmt(out_back, wu[1])

    far_rows(0)
    chunk = 32

    def edges_0(i, carry):
        at = pl.multiple_of(i * chunk, chunk)
        total = jnp.zeros((chunk, LATENT), F32)
        for k in range(DEGREE):
            rows = pl.ds(k * NODES + at, chunk)
            inner = r.base[rows, :]
            s = sigmoid(inner)
            value = inner * s
            total = total + value
            r.slope[rows, :] = (s + value * (1.0 - s)).astype(BF)
        r.agg[0, pl.ds(at, chunk), :] = total.astype(BF)
        return carry

    lax.fori_loop(0, NODES // chunk, edges_0, 0)
    r.mesh[1] = (r.mesh[0].astype(F32) + mm(r.agg[0], wu[0])).astype(BF)

    sender = send_rows(1)
    local_rows(1, sender)
    far_rows(1)

    def edges_1(i, carry):
        at = pl.multiple_of(i * chunk, chunk)
        total = jnp.zeros((chunk, LATENT), F32)
        back = jnp.zeros((chunk, LATENT), F32)
        given = r.ab[pl.ds(at, chunk), :]
        for k in range(DEGREE):
            rows = pl.ds(k * NODES + at, chunk)
            inner = r.base[rows, :]
            s = sigmoid(inner)
            value = inner * s
            total = total + value
            edge = given * (s + value * (1.0 - s))
            back = back + edge
            r.ib[rows, :] = edge.astype(BF)
        r.agg[1, pl.ds(at, chunk), :] = total.astype(BF)
        r.rb[pl.ds(at, chunk), :] = back.astype(BF)
        return carry

    lax.fori_loop(0, NODES // chunk, edges_1, 0)

    def edges_back(i, carry):
        at = pl.multiple_of(i * chunk, chunk)
        back = jnp.zeros((chunk, LATENT), F32)
        given = r.ab[pl.ds(at, chunk), :]
        for k in range(DEGREE):
            rows = pl.ds(k * NODES + at, chunk)
            edge = given * r.slope[rows, :].astype(F32)
            back = back + edge
            r.ib[rows, :] = edge.astype(BF)
        r.rb[pl.ds(at, chunk), :] = back.astype(BF)
        return carry

    def return_start(slot):
        pack(mm(r.t_far[...], r.ib[...]), r.fars[slot].source)
        far_start(slot)

    def return_local(layer):
        r.sback[...] = mm(r.t_loc[...], r.ib[...])
        r.lat[...] += mmt(r.rb[...], wr[layer])

    def return_end(slot, layer):
        far_wait(slot)
        unpack(r.fars[slot].target)
        sender_b = (r.sback[...] + mm(r.list_t[...], r.far[...])).astype(BF)
        r.lat[...] += mmt(sender_b, ws[layer])
        return sender_b

    return_start(2)
    mesh_last = (r.mesh[1].astype(F32) + mm(r.agg[1], wu[1])).astype(BF)
    r.mesh[2] = mesh_last
    r.mesh_ext[0:NODES, :] = mesh_last
    decode_pick = hot(column(decode_row) == iota((4 * HALO, NODES), 1))
    r.ns2[...] = mm(decode_pick, mesh_last).astype(BF)
    halo_mesh = r.mesh_ext.at[pl.ds(NODES, 4 * HALO)]
    near_start(2, r.ns2, halo_mesh)
    return_local(1)
    gradient(gd, 0, 256, turned(mesh_last), r.dback[...])
    gradient(ga, 0, 512, turned(r.ob[...]), r.agg[1])
    gradient(ga, 512, 512, turned(r.rb[...]), r.mesh[1])
    core_start(ga)
    near_wait(2, r.ns2, halo_mesh)
    sender_b1 = return_end(2, 1)

    out_back = r.lat[...].astype(BF)
    r.ob[...] = out_back
    r.ab[...] = mmt(out_back, wu[0])
    lax.fori_loop(0, NODES // chunk, edges_back, 0)
    return_start(3)
    core_wait(ga)
    band_start(ga)
    return_local(0)
    gradient(gb, 0, 512, turned(sender_b1), r.mesh[1])
    gradient(gb, 512, 512, turned(r.ob[...]), r.agg[0])
    gradient(gb, 1024, 512, turned(r.rb[...]), r.mesh[0])
    core_start(gb)
    decoded = mmt(r.dwp[...], r.mesh_ext[...]).astype(BF)
    forecast = r.xp[...].astype(F32) + mm(decoded, r.dec_t[...])
    out_pred[...] = forecast[0:CHANNELS, :].astype(BF)
    band_wait(ga)
    plane_start(ga)
    sender_b0 = return_end(3, 0)

    encode_back = (r.lat[...] * r.enc_slope[...]).astype(BF)
    input_back = mmt(encode_back, wn[...]).astype(BF)
    r.ns3[...] = mm(r.enc_t[GRID:, :], input_back).astype(BF)
    near_start(3, r.ns3, r.nr3)
    core_wait(gb)
    band_start(gb)
    r.gback[...] = mm(r.enc_t[0:GRID, :], input_back)
    gradient(gc, 0, 512, turned(sender_b0), r.mesh[0])
    gradient(gc, 512, 512, turned(encode_back), r.enc_in[...])
    core_start(gc)
    encode_spread = hot(encode_row == iota((GRID, 4 * HALO), 0))
    near_wait(3, r.ns3, r.nr3)
    r.gback[...] += mm(encode_spread, r.nr3[...])
    r.eb[...] = (r.gback[...] * r.gslope[...].astype(F32)).astype(BF)
    gradient(gd, 256, 256, turned(r.eb[...]), r.xp[...], mmt)
    core_start(gd)
    core_wait(gc)
    band_start(gc)
    core_wait(gd)
    band_start(gd)

    total = plane_wait(ga)

    def into(ref, layer=None):
        def write(j, value):
            if layer is None:
                ref[:, j * 128 : (j + 1) * 128] = value
            else:
                ref[layer, :, j * 128 : (j + 1) * 128] = value

        return write

    deliver(total, 0, into(out_refresh, 1))
    deliver(total, 512, into(out_target, 1))
    band_wait(gb)
    plane_start(gb)
    band_wait(gc)
    plane_start(gc)
    band_wait(gd)
    plane_start(gd)
    total = plane_wait(gb)
    deliver(total, 0, into(out_source, 1))
    deliver(total, 512, into(out_refresh, 0))
    deliver(total, 1024, into(out_target, 0))
    total = plane_wait(gc)
    deliver(total, 0, into(out_source, 0))
    deliver(total, 512, into(out_encode))
    total = plane_wait(gd)
    for ref, row in ((out_decode, 0), (out_embed, 8)):
        ref[:, 0:128] = total[row : row + 4, :]
        ref[:, 128:CHANNELS] = total[row + 4 : row + 8, 0 : CHANNELS - 128]


def on_device(
    lattice_feature_values,
    cotangent,
    embed_weight,
    encode_weight,
    sender_weight,
    receiver_weight,
    update_weight,
    decode_weight,
    encode_lists,
    encode_sources,
    mesh_lists,
    mesh_sources,
    decode_lists,
    decoder_edge_sources,
):
    spec, tree = jax.tree.flatten(scratch())
    whole = pl.BlockSpec(memory_space=pltpu.VMEM)
    shape = jax.ShapeDtypeStruct
    outs = pl.pallas_call(
        functools.partial(kernel, tree),
        out_shape=(
            shape((CHANNELS, GRID), BF),
            shape((4, CHANNELS), F32),
            shape((4, LATENT), F32),
            shape((2, 4, LATENT), F32),
            shape((2, 4, LATENT), F32),
            shape((2, 4, LATENT), F32),
            shape((4, CHANNELS), F32),
        ),
        in_specs=[whole] * 14,
        out_specs=(whole,) * 7,
        scratch_shapes=spec,
        compiler_params=pltpu.CompilerParams(
            collective_id=0, has_side_effects=True, vmem_limit_bytes=60 * 1024 * 1024
        ),
    )(
        lattice_feature_values.T,
        cotangent.T,
        embed_weight,
        encode_weight,
        sender_weight,
        receiver_weight,
        update_weight,
        decode_weight.T,
        encode_lists,
        encode_sources.T,
        mesh_lists.T,
        mesh_sources.T,
        decode_lists,
        decoder_edge_sources.T,
    )
    return (
        outs[0].T,
        outs[1].T,
        outs[2].T,
        outs[3].transpose(0, 2, 1),
        outs[4].transpose(0, 2, 1),
        outs[5].transpose(0, 2, 1),
        outs[6],
    )


def solution(mesh):
    return jax.shard_map(
        on_device,
        mesh=mesh,
        in_specs=(
            P(("lat", "lon"), None),
            P(("lat", "lon"), None),
            P(),
            P(),
            P(),
            P(),
            P(),
            P(),
            P(("lat", "lon"), None),
            P(("lat", "lon"), None),
            P(("lat", "lon"), None),
            P(("lat", "lon"), None),
            P(("lat", "lon"), None),
            P(("lat", "lon"), None),
        ),
        out_specs=(
            P(("lat", "lon"), None),
            P(None, ("lat", "lon")),
            P(None, ("lat", "lon")),
            P(None, None, ("lat", "lon")),
            P(None, None, ("lat", "lon")),
            P(None, None, ("lat", "lon")),
            P(("lat", "lon"), None),
        ),
        check_vma=False,
    )
```

```python
import functools

import jax
import jax.numpy as jnp
from jax import lax
from jax.experimental import pallas as pl
from jax.experimental.pallas import tpu as pltpu
from jax.sharding import PartitionSpec as P

BF = jnp.bfloat16
F32 = jnp.float32
MESH = pl.DeviceIdType.MESH

BANDS, SECTORS, PEERS = 4, 32, 128
LATENT, CHANNELS, PADDED = 512, 227, 256
GRID, NODES, HALO, SLOTS, DEGREE = 1024, 256, 64, 4, 8
EDGES = NODES * DEGREE
FAR = PEERS * SLOTS


def mm(a, b):
    return lax.dot_general(a, b, (((1,), (0,)), ((), ())), preferred_element_type=F32)


def mmt(a, b):
    return lax.dot_general(a, b, (((1,), (1,)), ((), ())), preferred_element_type=F32)


def tmm(a, b):
    return lax.dot_general(a, b, (((0,), (0,)), ((), ())), preferred_element_type=F32)


def sigmoid(v):
    return 0.5 * jnp.tanh(0.5 * v) + 0.5


def iota(shape, dim):
    return lax.broadcasted_iota(jnp.int32, shape, dim)


def hot(mask):
    return jnp.where(mask, 1.0, 0.0).astype(BF)


def column(row):
    return jnp.transpose(jnp.broadcast_to(row, (8, row.shape[1])))[:, :1]


class Refs:
    def __init__(self, named):
        for name, ref in named.items():
            if isinstance(ref, list):
                ref = [Refs(each) for each in ref]
            setattr(self, name, ref)


GROUPS = ((512, True), (512, False), (1024, True), (512, False), (512, True), (512, False), (512, True))


def scratch():
    vm = pltpu.VMEM
    sems = pltpu.SemaphoreType.DMA
    return dict(
        xp=vm((PADDED, GRID), BF),
        cp=vm((PADDED, GRID), BF),
        wep=vm((PADDED, LATENT), BF),
        dwp=vm((PADDED, LATENT), BF),
        grid_ext=vm((GRID + 4 * HALO, LATENT), BF),
        gslope=vm((GRID, LATENT), BF),
        enc_c=vm((NODES, GRID + 4 * HALO), BF),
        enc_t=vm((GRID + 4 * HALO, NODES), BF),
        dec_t=vm((NODES + 4 * HALO, GRID), BF),
        oh_loc=vm((EDGES, NODES), BF),
        oh_far=vm((EDGES, FAR), BF),
        t_loc=vm((NODES, EDGES), BF),
        t_far=vm((FAR, EDGES), BF),
        list_r=vm((FAR, NODES), BF),
        list_t=vm((NODES, FAR), BF),
        p_own=vm((2, NODES, LATENT), BF),
        p_oth=vm((2, NODES, LATENT), BF),
        enc_in=vm((NODES, LATENT), BF),
        enc_slope=vm((NODES, LATENT), F32),
        mesh=vm((3, NODES, LATENT), BF),
        agg=vm((2, NODES, LATENT), BF),
        base=vm((2, EDGES, LATENT), F32),
        slope=vm((EDGES, LATENT), BF),
        ib=vm((EDGES, LATENT), BF),
        rb=vm((NODES, LATENT), BF),
        ab=vm((NODES, LATENT), F32),
        ob=vm((NODES, LATENT), BF),
        lat=vm((NODES, LATENT), F32),
        dback=vm((NODES, PADDED), BF),
        dext=vm((NODES, PADDED), F32),
        sback=vm((NODES, LATENT), F32),
        gback=vm((GRID, LATENT), F32),
        eb=vm((GRID, LATENT), BF),
        far=vm((FAR, LATENT), BF),
        packed=vm((4 * FAR, 128), F32),
        ns0=vm((4 * HALO, LATENT), BF),
        ns1=vm((4 * HALO, PADDED), BF),
        nr1=vm((4 * HALO, PADDED), BF),
        ns2=vm((4 * HALO, LATENT), BF),
        mesh_ext=vm((NODES + 4 * HALO, LATENT), BF),
        ns3=vm((4 * HALO, LATENT), BF),
        nr3=vm((4 * HALO, LATENT), BF),
        near_sem=sems((4, 2)),
        far_sem=sems((4, 2)),
        fars=[dict(source=vm((4 * FAR, 128), BF), target=vm((4 * FAR, 128), BF)) for _ in range(4)],
        groups=[
            dict(
                own=vm((NODES, width), F32),
                sc=vm((NODES, width), BF),
                rc=vm((NODES, width), BF),
                sx=vm((NODES, width), BF),
                rx=vm((192 if along else NODES, width), BF),
                fp=vm((width // 2 if along else width // 8, 128), F32),
                sp=vm((width // 2 if along else width // 8, 128), BF),
                rp=vm((width // 2 if along else 3 * width // 32, 128), BF),
                sem=sems((3, 2)),
            )
            for width, along in GROUPS
        ],
    )


def kernel(tree, xt, ct, we, wn, ws, wr, wu, dwt, el, es, ml, ms, dl, ds_, *rest):
    out_pred, out_embed, out_encode, out_source, out_target, out_refresh, out_decode = rest[:7]
    r = Refs(jax.tree.unflatten(tree, rest[7:]))
    for each, (width, along) in zip(r.groups, GROUPS):
        each.along = along
    g_u1, g_r1, g_su, g_r0, g_s0, g_en, g_de = r.groups
    b = lax.axis_index("lat")
    c = lax.axis_index("lon")
    me = b * SECTORS + c
    core = lax.rem(c, 2)
    place = c // 2

    barrier = pltpu.get_barrier_semaphore()

    def greet(t, carry):
        u = lax.rem(b + t // SECTORS, BANDS)
        v = lax.rem(c + lax.rem(t, SECTORS), SECTORS)
        pl.semaphore_signal(barrier, inc=1, device_id=(u, v), device_id_type=MESH)
        return carry

    lax.fori_loop(1, PEERS, greet, 0)

    neighbours = (
        (b, lax.rem(c + SECTORS - 1, SECTORS)),
        (b, lax.rem(c + 1, SECTORS)),
        (lax.rem(b + BANDS - 1, BANDS), c),
        (lax.rem(b + 1, BANDS), c),
    )

    def drain(ref, sem):
        pltpu.make_async_copy(ref, ref, sem).wait()

    def near_start(i, source, target):
        for k in range(4):
            pltpu.make_async_remote_copy(
                source.at[pl.ds(k * HALO, HALO)],
                target.at[pl.ds((k ^ 1) * HALO, HALO)],
                r.near_sem.at[i, 0],
                r.near_sem.at[i, 1],
                device_id=neighbours[k],
                device_id_type=MESH,
            ).start()

    def near_wait(i, source, target):
        drain(target, r.near_sem.at[i, 1])
        drain(source, r.near_sem.at[i, 0])

    def far_start(i):
        source, target = r.fars[i].source, r.fars[i].target
        mine = pl.ds(pl.multiple_of(me * 16, 16), 16)

        def send(t, carry):
            u = lax.rem(b + lax.rem(t, BANDS), BANDS)
            v = lax.rem(c + t // BANDS, SECTORS)
            block = pl.ds(pl.multiple_of((u * SECTORS + v) * 16, 16), 16)
            pltpu.make_async_remote_copy(
                source.at[block],
                target.at[mine],
                r.far_sem.at[i, 0],
                r.far_sem.at[i, 1],
                device_id=(u, v),
                device_id_type=MESH,
            ).start()
            return carry

        lax.fori_loop(1, PEERS, send, 0)
        target[mine, :] = source[mine, :]

    def far_wait(i):
        rest_of = pl.ds(0, 16 * (PEERS - 1))
        drain(r.fars[i].target.at[rest_of], r.far_sem.at[i, 1])
        drain(r.fars[i].source.at[rest_of], r.far_sem.at[i, 0])

    packed = r.packed

    def pack(value, target):
        for i in range(SLOTS):
            for j in range(4):
                packed[pl.ds(4 * j + i, PEERS, stride=16), :] = value[
                    i * PEERS : (i + 1) * PEERS, j * 128 : (j + 1) * 128
                ]
        target[...] = packed[...].astype(BF)

    def unpack(source):
        packed[...] = source[...].astype(F32)
        for i in range(SLOTS):
            for j in range(4):
                r.far[i * PEERS : (i + 1) * PEERS, j * 128 : (j + 1) * 128] = packed[
                    pl.ds(4 * j + i, PEERS, stride=16), :
                ].astype(BF)

    def turned(g, value):
        order = 0 if g.along else 1
        return (
            mmt(r.p_own[order], value).astype(BF),
            mmt(r.p_oth[order], value).astype(BF),
        )

    def gradient(g, at, left, right):
        width = right.shape[1]
        sides = turned(g, left)
        g.own[:, at : at + width] = mm(sides[0], right)
        g.sc[:, at : at + width] = mm(sides[1], right).astype(BF)

    def core_start(g):
        pltpu.make_async_remote_copy(
            g.sc,
            g.rc,
            g.sem.at[0, 0],
            g.sem.at[0, 1],
            device_id=(b, c + 1 - 2 * core),
            device_id_type=MESH,
        ).start()

    def core_wait(g):
        drain(g.rc, g.sem.at[0, 1])
        drain(g.sc, g.sem.at[0, 0])
        total = g.own[...] + g.rc[...].astype(F32)
        g.own[...] = total
        g.sx[...] = total.astype(BF)

    def over_bands(g, hop, source, target, rows):
        for t in range(1, BANDS):
            u = lax.rem(b + t, BANDS)
            pltpu.make_async_remote_copy(
                source.at[pl.ds(pl.multiple_of(u * rows, 16), rows)],
                target.at[pl.ds((t - 1) * rows, rows)],
                g.sem.at[hop, 0],
                g.sem.at[hop, 1],
                device_id=(u, c),
                device_id_type=MESH,
            ).start()

    def over_plane(g, hop, source, target, rows):
        mine = pl.ds(pl.multiple_of(place * rows, 16), rows)

        def send(t, carry):
            q = lax.rem(place + t, 16)
            pltpu.make_async_remote_copy(
                source.at[pl.ds(pl.multiple_of(q * rows, 16), rows)],
                target.at[mine],
                g.sem.at[hop, 0],
                g.sem.at[hop, 1],
                device_id=(b, q * 2 + core),
                device_id_type=MESH,
            ).start()
            return carry

        lax.fori_loop(1, 16, send, 0)
        target[mine, :] = source[mine, :]

    def plane_sum(g, hop, source, target, rows):
        rest_of = pl.ds(0, 15 * rows)
        drain(target.at[rest_of], g.sem.at[hop, 1])
        drain(source.at[rest_of], g.sem.at[hop, 0])
        total = target[0:rows, :].astype(F32)
        for q in range(1, 16):
            total = total + target[q * rows : (q + 1) * rows, :].astype(F32)
        return total

    def band_sum(g, hop, source, target, rows, own):
        drain(target, g.sem.at[hop, 1])
        drain(source.at[pl.ds(0, 3 * rows)], g.sem.at[hop, 0])
        total = own[pl.ds(pl.multiple_of(b * rows, 8), rows), :]
        for t in range(3):
            total = total + target[t * rows : (t + 1) * rows, :].astype(F32)
        return total

    def first_start(g):
        core_wait(g)
        if g.along:
            over_bands(g, 1, g.sx, g.rx, 64)
        else:
            over_plane(g, 1, g.sx, g.rx, 16)

    def second_start(g):
        width = g.sc.shape[1]
        rows = width // 32
        if g.along:
            total = band_sum(g, 1, g.sx, g.rx, 64, g.own)
            for j in range(width // 128):
                for i in range(4):
                    g.fp[pl.ds(4 * j + i, 16, stride=rows), :] = total[
                        i * 16 : (i + 1) * 16, j * 128 : (j + 1) * 128
                    ]
        else:
            total = plane_sum(g, 1, g.sx, g.rx, 16)
            for u in range(4):
                for j in range(width // 128):
                    at = u * rows + 4 * j
                    g.fp[at : at + 4, :] = total[u * 4 : (u + 1) * 4, j * 128 : (j + 1) * 128]
        g.sp[...] = g.fp[...].astype(BF)
        if g.along:
            over_plane(g, 2, g.sp, g.rp, rows)
        else:
            over_bands(g, 2, g.sp, g.rp, rows)

    def finish(g):
        rows = g.sc.shape[1] // 32
        if g.along:
            return plane_sum(g, 2, g.sp, g.rp, rows)
        return band_sum(g, 2, g.sp, g.rp, rows, g.fp)

    def deliver(total, at, write):
        for j in range(4):
            row = 4 * (at // 128 + j)
            write(j, total[row : row + 4, :])

    for target, source in ((r.xp, xt), (r.cp, ct), (r.wep, we), (r.dwp, dwt)):
        target[224:256, :] = jnp.zeros((32, source.shape[1]), BF)
        target[0:CHANNELS, :] = source[...]

    def embed(i, carry):
        rows = pl.ds(pl.multiple_of(i * 256, 256), 256)
        inner = tmm(r.xp[:, rows], r.wep[...])
        s = sigmoid(inner)
        value = inner * s
        r.grid_ext[rows, :] = value.astype(BF)
        r.gslope[rows, :] = (s + value * (1.0 - s)).astype(BF)
        return carry

    lax.fori_loop(0, 4, embed, 0)

    def near_row(lists):
        return jnp.concatenate([lists[k : k + 1, :] for k in range(4)], axis=1)

    encode_row = near_row(el)
    decode_row = near_row(dl)
    encode_pick = hot(column(encode_row) == iota((4 * HALO, GRID), 1))
    r.ns0[...] = mm(encode_pick, r.grid_ext[0:GRID, :]).astype(BF)

    pl.semaphore_wait(barrier, PEERS - 1)
    halo_grid = r.grid_ext.at[pl.ds(GRID, 4 * HALO)]
    near_start(0, r.ns0, halo_grid)

    es_col = jnp.transpose(es[...])
    for part in range(5):
        where = iota((NODES, 256), 1) + part * 256
        total = jnp.zeros((NODES, 256), F32)
        for k in range(DEGREE):
            total = total + jnp.where(es_col[:, k : k + 1] == where, 1.0, 0.0)
        r.enc_c[:, part * 256 : (part + 1) * 256] = total.astype(BF)
    encode_local = mm(r.enc_c[:, 0:GRID], r.grid_ext[0:GRID, :])

    for i in range(SLOTS):
        row = ml[i : i + 1, :]
        r.list_r[i * PEERS : (i + 1) * PEERS, :] = hot(column(row) == iota((PEERS, NODES), 1))

    near_wait(0, r.ns0, halo_grid)
    encode_input = (encode_local + mm(r.enc_c[:, GRID:], r.grid_ext[GRID:, :])).astype(BF)
    r.enc_in[...] = encode_input
    encode_inner = mm(encode_input, wn[...])
    s = sigmoid(encode_inner)
    value = encode_inner * s
    r.mesh[0] = value.astype(BF)
    r.enc_slope[...] = s + value * (1.0 - s)

    def send_rows(layer):
        sender = mm(r.mesh[layer], ws[layer]).astype(BF)
        pack(mm(r.list_r[...], sender), r.fars[layer].source)
        far_start(layer)
        return sender

    def local_rows(layer, sender):
        receiver = mm(r.mesh[layer], wr[layer])
        for k in range(DEGREE):
            rows = slice(k * NODES, (k + 1) * NODES)
            r.base[layer, rows, :] = mm(r.oh_loc[rows, :], sender) + receiver

    def far_rows(layer):
        far_wait(layer)
        unpack(r.fars[layer].target)

        def add(k, carry):
            rows = pl.ds(pl.multiple_of(k * NODES, NODES), NODES)
            r.base[layer, rows, :] += mm(r.oh_far[rows, :], r.far[...])
            return carry

        lax.fori_loop(0, DEGREE, add, 0)

    sender = send_rows(0)

    def far_index(v):
        k = v - NODES
        return jnp.where(k >= 0, (k & 3) * PEERS + (k >> 2), -1)

    ms_row = ms[...]
    ms_col = jnp.transpose(ms_row)
    far_row = far_index(ms_row)
    far_col = far_index(ms_col)
    for k in range(DEGREE):
        rows = slice(k * NODES, (k + 1) * NODES)
        r.oh_loc[rows, :] = hot(ms_col[:, k : k + 1] == iota((NODES, NODES), 1))
        r.oh_far[rows, :] = hot(far_col[:, k : k + 1] == iota((NODES, FAR), 1))
    local_rows(0, sender)

    for part in range(2):
        where = iota((NODES, GRID), 0) + part * NODES
        total = jnp.zeros((NODES, GRID), F32)
        for k in range(3):
            total = total + jnp.where(ds_[k : k + 1, :] == where, 1.0, 0.0)
        r.dec_t[part * NODES : (part + 1) * NODES, :] = total.astype(BF)
    r.ns1[...] = mmt(r.dec_t[NODES:, :], r.cp[...]).astype(BF)
    near_start(1, r.ns1, r.nr1)
    r.dext[...] = mmt(r.dec_t[0:NODES, :], r.cp[...])

    far_rows(0)
    chunk = 32

    def edges_0(i, carry):
        at = pl.multiple_of(i * chunk, chunk)
        total = jnp.zeros((chunk, LATENT), F32)
        for k in range(DEGREE):
            inner = r.base[0, pl.ds(k * NODES + at, chunk), :]
            total = total + inner * sigmoid(inner)
        r.agg[0, pl.ds(at, chunk), :] = total.astype(BF)
        return carry

    lax.fori_loop(0, NODES // chunk, edges_0, 0)
    r.mesh[1] = (r.mesh[0].astype(F32) + mm(r.agg[0], wu[0])).astype(BF)

    sender = send_rows(1)
    local_rows(1, sender)

    decode_spread = hot(decode_row == iota((NODES, 4 * HALO), 0))
    near_wait(1, r.ns1, r.nr1)
    decode_back = (r.dext[...] + mm(decode_spread, r.nr1[...])).astype(BF)
    r.dback[...] = decode_back
    latent_back = mm(decode_back, r.dwp[...])
    r.lat[...] = latent_back
    out_back = latent_back.astype(BF)
    r.ob[...] = out_back
    r.ab[...] = mmt(out_back, wu[1])

    def slopes(i, carry):
        rows = pl.ds(pl.multiple_of(i * 64, 64), 64)
        inner = r.base[0, rows, :]
        s = sigmoid(inner)
        r.slope[rows, :] = (s + inner * s * (1.0 - s)).astype(BF)
        return carry

    lax.fori_loop(0, EDGES // 64, slopes, 0)
    for k in range(DEGREE):
        rows = slice(k * NODES, (k + 1) * NODES)
        r.t_loc[:, rows] = hot(ms_row[k : k + 1, :] == iota((NODES, NODES), 0))
        r.t_far[:, rows] = hot(far_row[k : k + 1, :] == iota((FAR, NODES), 0))
    for i in range(SLOTS):
        row = ml[i : i + 1, :]
        r.list_t[:, i * PEERS : (i + 1) * PEERS] = hot(row == iota((NODES, PEERS), 0))

    index = iota((NODES, LATENT), 0)
    named = iota((NODES, LATENT), 1)
    by_band = (index // 64) * 128 + (index % 16) * 8 + (index // 16) % 4
    by_place = (index // 16) * 8 + ((index // 4) % 4) * 128 + index % 4
    for order, first in enumerate((by_band, by_place)):
        r.p_own[order] = hot(first + core * 4 == named)
        r.p_oth[order] = hot(first + (1 - core) * 4 == named)

    far_rows(1)

    def edges_1(i, carry):
        at = pl.multiple_of(i * chunk, chunk)
        total = jnp.zeros((chunk, LATENT), F32)
        back = jnp.zeros((chunk, LATENT), F32)
        given = r.ab[pl.ds(at, chunk), :]
        for k in range(DEGREE):
            rows = pl.ds(k * NODES + at, chunk)
            inner = r.base[1, rows, :]
            s = sigmoid(inner)
            value = inner * s
            total = total + value
            edge = given * (s + value * (1.0 - s))
            back = back + edge
            r.ib[rows, :] = edge.astype(BF)
        r.agg[1, pl.ds(at, chunk), :] = total.astype(BF)
        r.rb[pl.ds(at, chunk), :] = back.astype(BF)
        return carry

    lax.fori_loop(0, NODES // chunk, edges_1, 0)

    def edges_back(i, carry):
        at = pl.multiple_of(i * chunk, chunk)
        back = jnp.zeros((chunk, LATENT), F32)
        given = r.ab[pl.ds(at, chunk), :]
        for k in range(DEGREE):
            rows = pl.ds(k * NODES + at, chunk)
            edge = given * r.slope[rows, :].astype(F32)
            back = back + edge
            r.ib[rows, :] = edge.astype(BF)
        r.rb[pl.ds(at, chunk), :] = back.astype(BF)
        return carry

    def return_start(slot):
        pack(mm(r.t_far[...], r.ib[...]), r.fars[slot].source)
        far_start(slot)

    def return_local(layer):
        r.sback[...] = mm(r.t_loc[...], r.ib[...])
        r.lat[...] += mmt(r.rb[...], wr[layer])

    def return_end(slot, layer):
        unpack(r.fars[slot].target)
        sender_b = (r.sback[...] + mm(r.list_t[...], r.far[...])).astype(BF)
        r.lat[...] += mmt(sender_b, ws[layer])
        return sender_b

    return_start(2)
    mesh_last = (r.mesh[1].astype(F32) + mm(r.agg[1], wu[1])).astype(BF)
    r.mesh[2] = mesh_last
    r.mesh_ext[0:NODES, :] = mesh_last
    decode_pick = hot(column(decode_row) == iota((4 * HALO, NODES), 1))
    r.ns2[...] = mm(decode_pick, mesh_last).astype(BF)
    halo_mesh = r.mesh_ext.at[pl.ds(NODES, 4 * HALO)]
    near_start(2, r.ns2, halo_mesh)
    return_local(1)
    gradient(g_u1, 0, r.ob[...], r.agg[1])
    core_start(g_u1)
    gradient(g_r1, 0, r.rb[...], r.mesh[1])
    core_start(g_r1)
    gradient(g_de, 0, mesh_last, r.dback[...])
    for part in range(5):
        where_t = iota((256, NODES), 0) + part * 256
        total_t = jnp.zeros((256, NODES), F32)
        for k in range(DEGREE):
            total_t = total_t + jnp.where(es[k : k + 1, :] == where_t, 1.0, 0.0)
        r.enc_t[part * 256 : (part + 1) * 256, :] = total_t.astype(BF)
    far_wait(2)
    first_start(g_u1)
    first_start(g_r1)
    sender_b1 = return_end(2, 1)

    out_back = r.lat[...].astype(BF)
    r.ob[...] = out_back
    r.ab[...] = mmt(out_back, wu[0])
    lax.fori_loop(0, NODES // chunk, edges_back, 0)
    return_start(3)
    return_local(0)
    gradient(g_su, 0, sender_b1, r.mesh[1])
    gradient(g_su, 512, r.ob[...], r.agg[0])
    core_start(g_su)
    gradient(g_r0, 0, r.rb[...], r.mesh[0])
    core_start(g_r0)
    near_wait(2, r.ns2, halo_mesh)
    decoded = mmt(r.dwp[...], r.mesh_ext[...]).astype(BF)
    forecast = r.xp[...].astype(F32) + mm(decoded, r.dec_t[...])
    out_pred[...] = forecast[0:CHANNELS, :].astype(BF)
    second_start(g_u1)
    second_start(g_r1)
    far_wait(3)
    first_start(g_su)
    first_start(g_r0)
    sender_b0 = return_end(3, 0)

    encode_back = (r.lat[...] * r.enc_slope[...]).astype(BF)
    input_back = mmt(encode_back, wn[...]).astype(BF)
    r.ns3[...] = mm(r.enc_t[GRID:, :], input_back).astype(BF)
    near_start(3, r.ns3, r.nr3)
    gradient(g_s0, 0, sender_b0, r.mesh[0])
    core_start(g_s0)
    gradient(g_en, 0, encode_back, r.enc_in[...])
    core_start(g_en)
    r.gback[...] = mm(r.enc_t[0:GRID, :], input_back)
    encode_spread = hot(encode_row == iota((GRID, 4 * HALO), 0))
    near_wait(3, r.ns3, r.nr3)
    first_start(g_s0)
    first_start(g_en)
    r.gback[...] += mm(encode_spread, r.nr3[...])
    r.eb[...] = (r.gback[...] * r.gslope[...].astype(F32)).astype(BF)
    across = mm(r.xp[...], r.eb[...]).astype(BF)
    g_de.own[:, 256:512] = mmt(r.p_own[0], across)
    g_de.sc[:, 256:512] = mmt(r.p_oth[0], across).astype(BF)
    core_start(g_de)

    def into(ref, layer=None):
        def write(j, value):
            if layer is None:
                ref[:, j * 128 : (j + 1) * 128] = value
            else:
                ref[layer, :, j * 128 : (j + 1) * 128] = value

        return write

    second_start(g_su)
    second_start(g_r0)
    first_start(g_de)
    second_start(g_s0)
    second_start(g_en)
    deliver(finish(g_u1), 0, into(out_refresh, 1))
    deliver(finish(g_r1), 0, into(out_target, 1))
    second_start(g_de)
    total = finish(g_su)
    deliver(total, 0, into(out_source, 1))
    deliver(total, 512, into(out_refresh, 0))
    deliver(finish(g_r0), 0, into(out_target, 0))
    deliver(finish(g_s0), 0, into(out_source, 0))
    deliver(finish(g_en), 0, into(out_encode))
    total = finish(g_de)
    for ref, row in ((out_decode, 0), (out_embed, 8)):
        ref[:, 0:128] = total[row : row + 4, :]
        ref[:, 128:CHANNELS] = total[row + 4 : row + 8, 0 : CHANNELS - 128]


def hand_over(*refs):
    for source, target in zip(refs[:7], refs[7:]):
        target[...] = source[...]


def on_device(
    lattice_feature_values,
    cotangent,
    embed_weight,
    encode_weight,
    sender_weight,
    receiver_weight,
    update_weight,
    decode_weight,
    encode_lists,
    encode_sources,
    mesh_lists,
    mesh_sources,
    decode_lists,
    decoder_edge_sources,
):
    spec, tree = jax.tree.flatten(scratch())
    whole = pl.BlockSpec(memory_space=pltpu.VMEM)
    shape = jax.ShapeDtypeStruct
    shapes = (
        shape((CHANNELS, GRID), BF),
        shape((4, CHANNELS), F32),
        shape((4, LATENT), F32),
        shape((2, 4, LATENT), F32),
        shape((2, 4, LATENT), F32),
        shape((2, 4, LATENT), F32),
        shape((4, CHANNELS), F32),
    )
    outs = pl.pallas_call(
        functools.partial(kernel, tree),
        out_shape=shapes,
        in_specs=[whole] * 14,
        out_specs=(whole,) * 7,
        scratch_shapes=spec,
        compiler_params=pltpu.CompilerParams(
            collective_id=0, has_side_effects=True, vmem_limit_bytes=60 * 1024 * 1024
        ),
    )(
        lattice_feature_values.T,
        cotangent.T,
        embed_weight,
        encode_weight,
        sender_weight,
        receiver_weight,
        update_weight,
        decode_weight.T,
        encode_lists,
        encode_sources.T,
        mesh_lists.T,
        mesh_sources.T,
        decode_lists,
        decoder_edge_sources.T,
    )
    outs = pl.pallas_call(
        hand_over,
        out_shape=shapes,
        in_specs=[whole] * 7,
        out_specs=(whole,) * 7,
    )(*outs)
    return (
        outs[0].T,
        outs[1].T,
        outs[2].T,
        outs[3].transpose(0, 2, 1),
        outs[4].transpose(0, 2, 1),
        outs[5].transpose(0, 2, 1),
        outs[6],
    )


def solution(mesh):
    return jax.shard_map(
        on_device,
        mesh=mesh,
        in_specs=(
            P(("lat", "lon"), None),
            P(("lat", "lon"), None),
            P(),
            P(),
            P(),
            P(),
            P(),
            P(),
            P(("lat", "lon"), None),
            P(("lat", "lon"), None),
            P(("lat", "lon"), None),
            P(("lat", "lon"), None),
            P(("lat", "lon"), None),
            P(("lat", "lon"), None),
        ),
        out_specs=(
            P(("lat", "lon"), None),
            P(None, ("lat", "lon")),
            P(None, ("lat", "lon")),
            P(None, None, ("lat", "lon")),
            P(None, None, ("lat", "lon")),
            P(None, None, ("lat", "lon")),
            P(("lat", "lon"), None),
        ),
        check_vma=False,
    )
```

```python
import functools

import jax
import jax.numpy as jnp
from jax import lax
from jax.experimental import pallas as pl
from jax.experimental.pallas import tpu as pltpu
from jax.sharding import PartitionSpec as P

BF = jnp.bfloat16
F32 = jnp.float32
MESH = pl.DeviceIdType.MESH

BANDS, SECTORS, PEERS = 4, 32, 128
LATENT, CHANNELS, PADDED = 512, 227, 256
GRID, NODES, HALO, SLOTS, DEGREE = 1024, 256, 64, 4, 8
EDGES = NODES * DEGREE
FAR = PEERS * SLOTS


def mm(a, b):
    return lax.dot_general(a, b, (((1,), (0,)), ((), ())), preferred_element_type=F32)


def mmt(a, b):
    return lax.dot_general(a, b, (((1,), (1,)), ((), ())), preferred_element_type=F32)


def tmm(a, b):
    return lax.dot_general(a, b, (((0,), (0,)), ((), ())), preferred_element_type=F32)


def sigmoid(v):
    return 0.5 * jnp.tanh(0.5 * v) + 0.5


def iota(shape, dim):
    return lax.broadcasted_iota(jnp.int32, shape, dim)


def hot(mask):
    return jnp.where(mask, 1.0, 0.0).astype(BF)


def column(row):
    return jnp.transpose(jnp.broadcast_to(row, (8, row.shape[1])))[:, :1]


class Refs:
    def __init__(self, named):
        for name, ref in named.items():
            if isinstance(ref, list):
                ref = [Refs(each) for each in ref]
            setattr(self, name, ref)


GROUPS = ((512, True), (512, False), (1024, True), (512, False), (512, True), (512, False), (512, True))


def scratch():
    vm = pltpu.VMEM
    sems = pltpu.SemaphoreType.DMA
    return dict(
        xp=vm((PADDED, GRID), BF),
        cp=vm((PADDED, GRID), BF),
        wep=vm((PADDED, LATENT), BF),
        dwp=vm((PADDED, LATENT), BF),
        grid_ext=vm((GRID + 4 * HALO, LATENT), BF),
        gslope=vm((GRID, LATENT), BF),
        enc_c=vm((NODES, GRID + 4 * HALO), BF),
        enc_t=vm((GRID + 4 * HALO, NODES), BF),
        dec_t=vm((NODES + 4 * HALO, GRID), BF),
        oh_loc=vm((EDGES, NODES), BF),
        oh_far=vm((EDGES, FAR), BF),
        t_loc=vm((NODES, EDGES), BF),
        t_far=vm((FAR, EDGES), BF),
        list_r=vm((FAR, NODES), BF),
        list_t=vm((NODES, FAR), BF),
        p_own=vm((2, NODES, LATENT), BF),
        p_oth=vm((2, NODES, LATENT), BF),
        enc_in=vm((NODES, LATENT), BF),
        enc_slope=vm((NODES, LATENT), F32),
        mesh=vm((3, NODES, LATENT), BF),
        agg=vm((2, NODES, LATENT), BF),
        base=vm((2, EDGES, LATENT), F32),
        slope=vm((EDGES, LATENT), BF),
        ib=vm((EDGES, LATENT), BF),
        rb=vm((NODES, LATENT), BF),
        back=vm((NODES, LATENT), F32),
        total=vm((NODES, LATENT), F32),
        ab=vm((NODES, LATENT), F32),
        ob=vm((NODES, LATENT), BF),
        lat=vm((NODES, LATENT), F32),
        dback=vm((NODES, PADDED), BF),
        dext=vm((NODES, PADDED), F32),
        sback=vm((NODES, LATENT), F32),
        gback=vm((GRID, LATENT), F32),
        eb=vm((GRID, LATENT), BF),
        far=vm((FAR, LATENT), BF),
        packed=vm((4 * FAR, 128), F32),
        ns0=vm((4 * HALO, LATENT), BF),
        ns1=vm((4 * HALO, PADDED), BF),
        nr1=vm((4 * HALO, PADDED), BF),
        ns2=vm((4 * HALO, LATENT), BF),
        mesh_ext=vm((NODES + 4 * HALO, LATENT), BF),
        ns3=vm((4 * HALO, LATENT), BF),
        nr3=vm((4 * HALO, LATENT), BF),
        near_sem=sems((4, 2)),
        far_sem=sems((4, 2)),
        entered=pltpu.SemaphoreType.REGULAR,
        cot=vm((CHANNELS, GRID), BF),
        wn=vm((LATENT, LATENT), BF),
        ws=vm((2, LATENT, LATENT), BF),
        wr=vm((2, LATENT, LATENT), BF),
        wu=vm((2, LATENT, LATENT), BF),
        load_sem=sems((5,)),
        fars=[dict(source=vm((4 * FAR, 128), BF), target=vm((4 * FAR, 128), BF)) for _ in range(4)],
        groups=[
            dict(
                own=vm((NODES, width), F32),
                sc=vm((NODES, width), BF),
                rc=vm((NODES, width), BF),
                sx=vm((NODES, width), BF),
                rx=vm((192 if along else NODES, width), BF),
                fp=vm((width // 2 if along else width // 8, 128), F32),
                sp=vm((width // 2 if along else width // 8, 128), BF),
                rp=vm((width // 2 if along else 3 * width // 32, 128), BF),
                sem=sems((3, 2)),
            )
            for width, along in GROUPS
        ],
    )


def kernel(tree, xt, ct_far, we, wn_far, ws_far, wr_far, wu_far, dwt, el, es, ml, ms, dl, ds_, *rest):
    out_pred, out_embed, out_encode, out_source, out_target, out_refresh, out_decode = rest[:7]
    r = Refs(jax.tree.unflatten(tree, rest[7:]))
    for each, (width, along) in zip(r.groups, GROUPS):
        each.along = along
    g_u1, g_r1, g_su, g_r0, g_s0, g_en, g_de = r.groups
    b = lax.axis_index("lat")
    c = lax.axis_index("lon")
    me = b * SECTORS + c
    core = lax.rem(c, 2)
    place = c // 2

    barrier = pltpu.get_barrier_semaphore()

    def greet(t, carry):
        v = lax.rem(c + t, SECTORS)
        pl.semaphore_signal(barrier, inc=1, device_id=(b, v), device_id_type=MESH)
        return carry

    lax.fori_loop(1, SECTORS, greet, 0)

    def greet_bands(semaphore):
        for t in range(1, BANDS):
            u = lax.rem(b + t, BANDS)
            pl.semaphore_signal(semaphore, inc=1, device_id=(u, c), device_id_type=MESH)

    greet_bands(barrier)

    neighbours = (
        (b, lax.rem(c + SECTORS - 1, SECTORS)),
        (b, lax.rem(c + 1, SECTORS)),
        (lax.rem(b + BANDS - 1, BANDS), c),
        (lax.rem(b + 1, BANDS), c),
    )

    def drain(ref, sem):
        pltpu.make_async_copy(ref, ref, sem).wait()

    def near_start(i, source, target):
        for k in range(4):
            pltpu.make_async_remote_copy(
                source.at[pl.ds(k * HALO, HALO)],
                target.at[pl.ds((k ^ 1) * HALO, HALO)],
                r.near_sem.at[i, 0],
                r.near_sem.at[i, 1],
                device_id=neighbours[k],
                device_id_type=MESH,
            ).start()

    def near_wait(i, source, target):
        drain(target, r.near_sem.at[i, 1])
        drain(source, r.near_sem.at[i, 0])

    def far_start(i):
        source, target = r.fars[i].source, r.fars[i].target
        mine = pl.ds(pl.multiple_of(me * 16, 16), 16)

        def send(t, carry):
            u = lax.rem(b + lax.rem(t, BANDS), BANDS)
            v = lax.rem(c + t // BANDS, SECTORS)
            block = pl.ds(pl.multiple_of((u * SECTORS + v) * 16, 16), 16)
            pltpu.make_async_remote_copy(
                source.at[block],
                target.at[mine],
                r.far_sem.at[i, 0],
                r.far_sem.at[i, 1],
                device_id=(u, v),
                device_id_type=MESH,
            ).start()
            return carry

        lax.fori_loop(1, PEERS, send, 0)
        target[mine, :] = source[mine, :]

    def far_wait(i):
        rest_of = pl.ds(0, 16 * (PEERS - 1))
        drain(r.fars[i].target.at[rest_of], r.far_sem.at[i, 1])
        drain(r.fars[i].source.at[rest_of], r.far_sem.at[i, 0])

    packed = r.packed
    chunk = 32

    def pack(value, target):
        for i in range(SLOTS):
            for j in range(4):
                packed[pl.ds(4 * j + i, PEERS, stride=16), :] = value[
                    i * PEERS : (i + 1) * PEERS, j * 128 : (j + 1) * 128
                ]
        target[...] = packed[...].astype(BF)

    def unpack(source):
        packed[...] = source[...].astype(F32)
        for i in range(SLOTS):
            for j in range(4):
                r.far[i * PEERS : (i + 1) * PEERS, j * 128 : (j + 1) * 128] = packed[
                    pl.ds(4 * j + i, PEERS, stride=16), :
                ].astype(BF)

    def turned(g, value):
        order = 0 if g.along else 1
        return (
            mmt(r.p_own[order], value).astype(BF),
            mmt(r.p_oth[order], value).astype(BF),
        )

    def gradient(g, at, left, right):
        width = right.shape[1]
        sides = turned(g, left)
        g.own[:, at : at + width] = mm(sides[0], right)
        g.sc[:, at : at + width] = mm(sides[1], right).astype(BF)

    def core_start(g):
        pltpu.make_async_remote_copy(
            g.sc,
            g.rc,
            g.sem.at[0, 0],
            g.sem.at[0, 1],
            device_id=(b, c + 1 - 2 * core),
            device_id_type=MESH,
        ).start()

    def core_wait(g):
        drain(g.rc, g.sem.at[0, 1])
        drain(g.sc, g.sem.at[0, 0])
        total = g.own[...] + g.rc[...].astype(F32)
        g.own[...] = total
        g.sx[...] = total.astype(BF)

    def over_bands(g, hop, source, target, rows):
        for t in range(1, BANDS):
            u = lax.rem(b + t, BANDS)
            pltpu.make_async_remote_copy(
                source.at[pl.ds(pl.multiple_of(u * rows, 16), rows)],
                target.at[pl.ds((t - 1) * rows, rows)],
                g.sem.at[hop, 0],
                g.sem.at[hop, 1],
                device_id=(u, c),
                device_id_type=MESH,
            ).start()

    def over_plane(g, hop, source, target, rows):
        mine = pl.ds(pl.multiple_of(place * rows, 16), rows)

        def send(t, carry):
            q = lax.rem(place + t, 16)
            pltpu.make_async_remote_copy(
                source.at[pl.ds(pl.multiple_of(q * rows, 16), rows)],
                target.at[mine],
                g.sem.at[hop, 0],
                g.sem.at[hop, 1],
                device_id=(b, q * 2 + core),
                device_id_type=MESH,
            ).start()
            return carry

        lax.fori_loop(1, 16, send, 0)
        target[mine, :] = source[mine, :]

    def plane_sum(g, hop, source, target, rows):
        rest_of = pl.ds(0, 15 * rows)
        drain(target.at[rest_of], g.sem.at[hop, 1])
        drain(source.at[rest_of], g.sem.at[hop, 0])
        total = target[0:rows, :].astype(F32)
        for q in range(1, 16):
            total = total + target[q * rows : (q + 1) * rows, :].astype(F32)
        return total

    def band_sum(g, hop, source, target, rows, own):
        drain(target, g.sem.at[hop, 1])
        drain(source.at[pl.ds(0, 3 * rows)], g.sem.at[hop, 0])
        total = own[pl.ds(pl.multiple_of(b * rows, 8), rows), :]
        for t in range(3):
            total = total + target[t * rows : (t + 1) * rows, :].astype(F32)
        return total

    def first_start(g):
        core_wait(g)
        if g.along:
            over_bands(g, 1, g.sx, g.rx, 64)
        else:
            over_plane(g, 1, g.sx, g.rx, 16)

    def second_start(g):
        width = g.sc.shape[1]
        rows = width // 32
        if g.along:
            total = band_sum(g, 1, g.sx, g.rx, 64, g.own)
            for j in range(width // 128):
                for i in range(4):
                    g.fp[pl.ds(4 * j + i, 16, stride=rows), :] = total[
                        i * 16 : (i + 1) * 16, j * 128 : (j + 1) * 128
                    ]
        else:
            total = plane_sum(g, 1, g.sx, g.rx, 16)
            for u in range(4):
                for j in range(width // 128):
                    at = u * rows + 4 * j
                    g.fp[at : at + 4, :] = total[u * 4 : (u + 1) * 4, j * 128 : (j + 1) * 128]
        g.sp[...] = g.fp[...].astype(BF)
        if g.along:
            over_plane(g, 2, g.sp, g.rp, rows)
        else:
            over_bands(g, 2, g.sp, g.rp, rows)

    def finish(g):
        rows = g.sc.shape[1] // 32
        if g.along:
            return plane_sum(g, 2, g.sp, g.rp, rows)
        return band_sum(g, 2, g.sp, g.rp, rows, g.fp)

    def deliver(total, at, write):
        for j in range(4):
            row = 4 * (at // 128 + j)
            write(j, total[row : row + 4, :])

    wn, ws, wr, wu = r.wn, r.ws, r.wr, r.wu
    loads = [
        pltpu.make_async_copy(source, target, r.load_sem.at[i])
        for i, (source, target) in enumerate(
            ((wn_far, wn), (ws_far, ws), (wr_far, wr), (wu_far, wu), (ct_far, r.cot))
        )
    ]
    for each in loads:
        each.start()

    for target, source in ((r.xp, xt), (r.wep, we), (r.dwp, dwt)):
        target[224:256, :] = jnp.zeros((32, source.shape[1]), BF)
        target[0:CHANNELS, :] = source[...]

    def embed(i, carry):
        rows = pl.ds(pl.multiple_of(i * 256, 256), 256)
        inner = tmm(r.xp[:, rows], r.wep[...])
        s = sigmoid(inner)
        value = inner * s
        r.grid_ext[rows, :] = value.astype(BF)
        r.gslope[rows, :] = (s + value * (1.0 - s)).astype(BF)
        return carry

    lax.fori_loop(0, 4, embed, 0)

    def near_row(lists):
        return jnp.concatenate([lists[k : k + 1, :] for k in range(4)], axis=1)

    encode_row = near_row(el)
    decode_row = near_row(dl)
    encode_pick = hot(column(encode_row) == iota((4 * HALO, GRID), 1))
    r.ns0[...] = mm(encode_pick, r.grid_ext[0:GRID, :]).astype(BF)

    pl.semaphore_wait(barrier, SECTORS - 1 + BANDS - 1)
    greet_bands(r.entered)
    halo_grid = r.grid_ext.at[pl.ds(GRID, 4 * HALO)]
    near_start(0, r.ns0, halo_grid)
    for each in loads:
        each.wait()
    r.cp[224:256, :] = jnp.zeros((32, GRID), BF)
    r.cp[0:CHANNELS, :] = r.cot[...]

    es_col = jnp.transpose(es[...])
    for part in range(5):
        where = iota((NODES, 256), 1) + part * 256
        total = jnp.zeros((NODES, 256), F32)
        for k in range(DEGREE):
            total = total + jnp.where(es_col[:, k : k + 1] == where, 1.0, 0.0)
        r.enc_c[:, part * 256 : (part + 1) * 256] = total.astype(BF)
    encode_local = mm(r.enc_c[:, 0:GRID], r.grid_ext[0:GRID, :])

    for i in range(SLOTS):
        row = ml[i : i + 1, :]
        r.list_r[i * PEERS : (i + 1) * PEERS, :] = hot(column(row) == iota((PEERS, NODES), 1))

    near_wait(0, r.ns0, halo_grid)
    encode_input = (encode_local + mm(r.enc_c[:, GRID:], r.grid_ext[GRID:, :])).astype(BF)
    r.enc_in[...] = encode_input
    encode_inner = mm(encode_input, wn[...])
    s = sigmoid(encode_inner)
    value = encode_inner * s
    r.mesh[0] = value.astype(BF)
    r.enc_slope[...] = s + value * (1.0 - s)

    def send_rows(layer):
        sender = mm(r.mesh[layer], ws[layer]).astype(BF)
        pack(mm(r.list_r[...], sender), r.fars[layer].source)
        far_start(layer)
        return sender

    def local_rows(layer, sender):
        receiver = mm(r.mesh[layer], wr[layer])
        for k in range(DEGREE):
            rows = slice(k * NODES, (k + 1) * NODES)
            r.base[layer, rows, :] = mm(r.oh_loc[rows, :], sender) + receiver

    def far_rows(layer, edge):
        far_wait(layer)
        unpack(r.fars[layer].target)
        r.total[...] = jnp.zeros((NODES, LATENT), F32)

        def add(k, carry):
            at = pl.multiple_of(k * NODES, NODES)
            rows = pl.ds(at, NODES)
            far = mm(r.oh_far[rows, :], r.far[...])
            for h in range(NODES // chunk):
                part = slice(h * chunk, (h + 1) * chunk)
                rows = pl.ds(at + h * chunk, chunk)
                inner = r.base[layer, rows, :] + far[part, :]
                s = sigmoid(inner)
                value = inner * s
                r.total[part, :] += value
                edge(inner, s, value, part, rows)
            return carry

        lax.fori_loop(0, DEGREE, add, 0)
        r.agg[layer] = r.total[...].astype(BF)

    pl.semaphore_wait(r.entered, BANDS - 1)
    sender = send_rows(0)

    def far_index(v):
        k = v - NODES
        return jnp.where(k >= 0, (k & 3) * PEERS + (k >> 2), -1)

    ms_row = ms[...]
    ms_col = jnp.transpose(ms_row)
    far_row = far_index(ms_row)
    far_col = far_index(ms_col)
    for k in range(DEGREE):
        rows = slice(k * NODES, (k + 1) * NODES)
        r.oh_loc[rows, :] = hot(ms_col[:, k : k + 1] == iota((NODES, NODES), 1))
        r.oh_far[rows, :] = hot(far_col[:, k : k + 1] == iota((NODES, FAR), 1))
    local_rows(0, sender)

    for part in range(2):
        where = iota((NODES, GRID), 0) + part * NODES
        total = jnp.zeros((NODES, GRID), F32)
        for k in range(3):
            total = total + jnp.where(ds_[k : k + 1, :] == where, 1.0, 0.0)
        r.dec_t[part * NODES : (part + 1) * NODES, :] = total.astype(BF)
    r.ns1[...] = mmt(r.dec_t[NODES:, :], r.cp[...]).astype(BF)
    near_start(1, r.ns1, r.nr1)
    r.dext[...] = mmt(r.dec_t[0:NODES, :], r.cp[...])

    def keep(inner, s, value, part, rows):
        r.base[0, rows, :] = inner

    far_rows(0, keep)
    r.mesh[1] = (r.mesh[0].astype(F32) + mm(r.agg[0], wu[0])).astype(BF)

    sender = send_rows(1)
    local_rows(1, sender)

    decode_spread = hot(decode_row == iota((NODES, 4 * HALO), 0))
    near_wait(1, r.ns1, r.nr1)
    decode_back = (r.dext[...] + mm(decode_spread, r.nr1[...])).astype(BF)
    r.dback[...] = decode_back
    latent_back = mm(decode_back, r.dwp[...])
    r.lat[...] = latent_back
    out_back = latent_back.astype(BF)
    r.ob[...] = out_back
    r.ab[...] = mmt(out_back, wu[1])

    def slopes(i, carry):
        rows = pl.ds(pl.multiple_of(i * 64, 64), 64)
        inner = r.base[0, rows, :]
        s = sigmoid(inner)
        r.slope[rows, :] = (s + inner * s * (1.0 - s)).astype(BF)
        return carry

    lax.fori_loop(0, EDGES // 64, slopes, 0)
    for k in range(DEGREE):
        rows = slice(k * NODES, (k + 1) * NODES)
        r.t_loc[:, rows] = hot(ms_row[k : k + 1, :] == iota((NODES, NODES), 0))
        r.t_far[:, rows] = hot(far_row[k : k + 1, :] == iota((FAR, NODES), 0))
    for i in range(SLOTS):
        row = ml[i : i + 1, :]
        r.list_t[:, i * PEERS : (i + 1) * PEERS] = hot(row == iota((NODES, PEERS), 0))

    index = iota((NODES, LATENT), 0)
    named = iota((NODES, LATENT), 1)
    by_band = (index // 64) * 128 + (index % 16) * 8 + (index // 16) % 4
    by_place = (index // 16) * 8 + ((index // 4) % 4) * 128 + index % 4
    for order, first in enumerate((by_band, by_place)):
        r.p_own[order] = hot(first + core * 4 == named)
        r.p_oth[order] = hot(first + (1 - core) * 4 == named)

    r.back[...] = jnp.zeros((NODES, LATENT), F32)

    def turn(inner, s, value, part, rows):
        back = r.ab[part, :] * (s + value * (1.0 - s))
        r.back[part, :] += back
        r.ib[rows, :] = back.astype(BF)

    far_rows(1, turn)
    r.rb[...] = r.back[...].astype(BF)

    def edges_back(i, carry):
        at = pl.multiple_of(i * chunk, chunk)
        back = jnp.zeros((chunk, LATENT), F32)
        given = r.ab[pl.ds(at, chunk), :]
        for k in range(DEGREE):
            rows = pl.ds(k * NODES + at, chunk)
            edge = given * r.slope[rows, :].astype(F32)
            back = back + edge
            r.ib[rows, :] = edge.astype(BF)
        r.rb[pl.ds(at, chunk), :] = back.astype(BF)
        return carry

    def return_start(slot):
        pack(mm(r.t_far[...], r.ib[...]), r.fars[slot].source)
        far_start(slot)

    def return_local(layer):
        r.sback[...] = mm(r.t_loc[...], r.ib[...])
        r.lat[...] += mmt(r.rb[...], wr[layer])

    def return_end(slot, layer):
        unpack(r.fars[slot].target)
        sender_b = (r.sback[...] + mm(r.list_t[...], r.far[...])).astype(BF)
        r.lat[...] += mmt(sender_b, ws[layer])
        return sender_b

    return_start(2)
    mesh_last = (r.mesh[1].astype(F32) + mm(r.agg[1], wu[1])).astype(BF)
    r.mesh[2] = mesh_last
    r.mesh_ext[0:NODES, :] = mesh_last
    decode_pick = hot(column(decode_row) == iota((4 * HALO, NODES), 1))
    r.ns2[...] = mm(decode_pick, mesh_last).astype(BF)
    halo_mesh = r.mesh_ext.at[pl.ds(NODES, 4 * HALO)]
    near_start(2, r.ns2, halo_mesh)
    return_local(1)
    gradient(g_u1, 0, r.ob[...], r.agg[1])
    core_start(g_u1)
    gradient(g_r1, 0, r.rb[...], r.mesh[1])
    core_start(g_r1)
    gradient(g_de, 0, mesh_last, r.dback[...])
    for part in range(5):
        where_t = iota((256, NODES), 0) + part * 256
        total_t = jnp.zeros((256, NODES), F32)
        for k in range(DEGREE):
            total_t = total_t + jnp.where(es[k : k + 1, :] == where_t, 1.0, 0.0)
        r.enc_t[part * 256 : (part + 1) * 256, :] = total_t.astype(BF)
    first_start(g_u1)
    first_start(g_r1)
    far_wait(2)
    sender_b1 = return_end(2, 1)

    out_back = r.lat[...].astype(BF)
    r.ob[...] = out_back
    r.ab[...] = mmt(out_back, wu[0])
    lax.fori_loop(0, NODES // chunk, edges_back, 0)
    return_start(3)
    return_local(0)
    gradient(g_su, 0, sender_b1, r.mesh[1])
    gradient(g_su, 512, r.ob[...], r.agg[0])
    core_start(g_su)
    gradient(g_r0, 0, r.rb[...], r.mesh[0])
    core_start(g_r0)
    near_wait(2, r.ns2, halo_mesh)
    decoded = mmt(r.dwp[...], r.mesh_ext[...]).astype(BF)
    forecast = r.xp[...].astype(F32) + mm(decoded, r.dec_t[...])
    out_pred[...] = forecast[0:CHANNELS, :].astype(BF)
    first_start(g_su)
    first_start(g_r0)
    second_start(g_u1)
    second_start(g_r1)
    far_wait(3)
    sender_b0 = return_end(3, 0)

    encode_back = (r.lat[...] * r.enc_slope[...]).astype(BF)
    input_back = mmt(encode_back, wn[...]).astype(BF)
    r.ns3[...] = mm(r.enc_t[GRID:, :], input_back).astype(BF)
    near_start(3, r.ns3, r.nr3)
    gradient(g_s0, 0, sender_b0, r.mesh[0])
    core_start(g_s0)
    gradient(g_en, 0, encode_back, r.enc_in[...])
    core_start(g_en)
    r.gback[...] = mm(r.enc_t[0:GRID, :], input_back)
    encode_spread = hot(encode_row == iota((GRID, 4 * HALO), 0))
    first_start(g_s0)
    first_start(g_en)
    second_start(g_su)
    second_start(g_r0)
    near_wait(3, r.ns3, r.nr3)
    r.gback[...] += mm(encode_spread, r.nr3[...])
    r.eb[...] = (r.gback[...] * r.gslope[...].astype(F32)).astype(BF)
    across = mm(r.xp[...], r.eb[...]).astype(BF)
    g_de.own[:, 256:512] = mmt(r.p_own[0], across)
    g_de.sc[:, 256:512] = mmt(r.p_oth[0], across).astype(BF)
    core_start(g_de)

    def into(ref, layer=None):
        def write(j, value):
            if layer is None:
                ref[:, j * 128 : (j + 1) * 128] = value
            else:
                ref[layer, :, j * 128 : (j + 1) * 128] = value

        return write

    first_start(g_de)
    second_start(g_s0)
    second_start(g_en)
    deliver(finish(g_u1), 0, into(out_refresh, 1))
    deliver(finish(g_r1), 0, into(out_target, 1))
    second_start(g_de)
    total = finish(g_su)
    deliver(total, 0, into(out_source, 1))
    deliver(total, 512, into(out_refresh, 0))
    deliver(finish(g_r0), 0, into(out_target, 0))
    deliver(finish(g_s0), 0, into(out_source, 0))
    deliver(finish(g_en), 0, into(out_encode))
    total = finish(g_de)
    for ref, row in ((out_decode, 0), (out_embed, 8)):
        ref[:, 0:128] = total[row : row + 4, :]
        ref[:, 128:CHANNELS] = total[row + 4 : row + 8, 0 : CHANNELS - 128]


def hand_over(*refs):
    for source, target in zip(refs[:7], refs[7:]):
        target[...] = source[...]


def on_device(
    lattice_feature_values,
    cotangent,
    embed_weight,
    encode_weight,
    sender_weight,
    receiver_weight,
    update_weight,
    decode_weight,
    encode_lists,
    encode_sources,
    mesh_lists,
    mesh_sources,
    decode_lists,
    decoder_edge_sources,
):
    spec, tree = jax.tree.flatten(scratch())
    whole = pl.BlockSpec(memory_space=pltpu.VMEM)
    far = pl.BlockSpec(memory_space=pl.ANY)
    shape = jax.ShapeDtypeStruct
    shapes = (
        shape((CHANNELS, GRID), BF),
        shape((4, CHANNELS), F32),
        shape((4, LATENT), F32),
        shape((2, 4, LATENT), F32),
        shape((2, 4, LATENT), F32),
        shape((2, 4, LATENT), F32),
        shape((4, CHANNELS), F32),
    )
    outs = pl.pallas_call(
        functools.partial(kernel, tree),
        out_shape=shapes,
        in_specs=[whole, far, whole, far, far, far, far] + [whole] * 7,
        out_specs=(whole,) * 7,
        scratch_shapes=spec,
        compiler_params=pltpu.CompilerParams(
            collective_id=0, has_side_effects=True, vmem_limit_bytes=60 * 1024 * 1024
        ),
    )(
        lattice_feature_values.T,
        cotangent.T,
        embed_weight,
        encode_weight,
        sender_weight,
        receiver_weight,
        update_weight,
        decode_weight.T,
        encode_lists,
        encode_sources.T,
        mesh_lists.T,
        mesh_sources.T,
        decode_lists,
        decoder_edge_sources.T,
    )
    outs = pl.pallas_call(
        hand_over,
        out_shape=shapes,
        in_specs=[whole] * 7,
        out_specs=(whole,) * 7,
    )(*outs)
    return (
        outs[0].T,
        outs[1].T,
        outs[2].T,
        outs[3].transpose(0, 2, 1),
        outs[4].transpose(0, 2, 1),
        outs[5].transpose(0, 2, 1),
        outs[6],
    )


def solution(mesh):
    return jax.shard_map(
        on_device,
        mesh=mesh,
        in_specs=(
            P(("lat", "lon"), None),
            P(("lat", "lon"), None),
            P(),
            P(),
            P(),
            P(),
            P(),
            P(),
            P(("lat", "lon"), None),
            P(("lat", "lon"), None),
            P(("lat", "lon"), None),
            P(("lat", "lon"), None),
            P(("lat", "lon"), None),
            P(("lat", "lon"), None),
        ),
        out_specs=(
            P(("lat", "lon"), None),
            P(None, ("lat", "lon")),
            P(None, ("lat", "lon")),
            P(None, None, ("lat", "lon")),
            P(None, None, ("lat", "lon")),
            P(None, None, ("lat", "lon")),
            P(("lat", "lon"), None),
        ),
        check_vma=False,
    )
```

```python
import functools

import jax
import jax.numpy as jnp
from jax import lax
from jax.experimental import pallas as pl
from jax.experimental.pallas import tpu as pltpu
from jax.sharding import PartitionSpec as P

BF = jnp.bfloat16
F32 = jnp.float32
MESH = pl.DeviceIdType.MESH

BANDS, SECTORS, PEERS = 4, 32, 128
LATENT, CHANNELS, PADDED = 512, 227, 256
GRID, NODES, HALO, SLOTS, DEGREE = 1024, 256, 64, 4, 8
EDGES = NODES * DEGREE
FAR = PEERS * SLOTS


def mm(a, b):
    return lax.dot_general(a, b, (((1,), (0,)), ((), ())), preferred_element_type=F32)


def mmt(a, b):
    return lax.dot_general(a, b, (((1,), (1,)), ((), ())), preferred_element_type=F32)


def tmm(a, b):
    return lax.dot_general(a, b, (((0,), (0,)), ((), ())), preferred_element_type=F32)


def sigmoid(v):
    return 0.5 * jnp.tanh(0.5 * v) + 0.5


def iota(shape, dim):
    return lax.broadcasted_iota(jnp.int32, shape, dim)


def hot(mask):
    return jnp.where(mask, 1.0, 0.0).astype(BF)


def column(row):
    return jnp.transpose(jnp.broadcast_to(row, (8, row.shape[1])))[:, :1]


class Refs:
    def __init__(self, named):
        for name, ref in named.items():
            if isinstance(ref, list):
                ref = [Refs(each) for each in ref]
            setattr(self, name, ref)


GROUPS = ((512, True), (512, False), (1024, True), (512, False), (512, True), (512, False), (512, True))


def scratch():
    vm = pltpu.VMEM
    sems = pltpu.SemaphoreType.DMA
    return dict(
        xp=vm((PADDED, GRID), BF),
        cp=vm((PADDED, GRID), BF),
        wep=vm((PADDED, LATENT), BF),
        dwp=vm((PADDED, LATENT), BF),
        grid_ext=vm((GRID + 4 * HALO, LATENT), BF),
        gslope=vm((GRID, LATENT), BF),
        enc_c=vm((NODES, GRID + 4 * HALO), BF),
        enc_t=vm((GRID + 4 * HALO, NODES), BF),
        dec_t=vm((NODES + 4 * HALO, GRID), BF),
        oh_loc=vm((EDGES, NODES), BF),
        oh_far=vm((EDGES, FAR), BF),
        t_loc=vm((NODES, EDGES), BF),
        t_far=vm((FAR, EDGES), BF),
        list_r=vm((FAR, NODES), BF),
        list_t=vm((NODES, FAR), BF),
        p_own=vm((2, NODES, LATENT), BF),
        p_oth=vm((2, NODES, LATENT), BF),
        enc_in=vm((NODES, LATENT), BF),
        enc_slope=vm((NODES, LATENT), F32),
        mesh=vm((3, NODES, LATENT), BF),
        agg=vm((2, NODES, LATENT), BF),
        base=vm((2, EDGES, LATENT), F32),
        slope=vm((EDGES, LATENT), BF),
        ib=vm((EDGES, LATENT), BF),
        rb=vm((NODES, LATENT), BF),
        back=vm((NODES, LATENT), F32),
        total=vm((NODES, LATENT), F32),
        ab=vm((NODES, LATENT), F32),
        ob=vm((NODES, LATENT), BF),
        lat=vm((NODES, LATENT), F32),
        dback=vm((NODES, PADDED), BF),
        dext=vm((NODES, PADDED), F32),
        sback=vm((NODES, LATENT), F32),
        gback=vm((GRID, LATENT), F32),
        eb=vm((GRID, LATENT), BF),
        far=vm((FAR, LATENT), BF),
        packed=vm((4 * FAR, 128), F32),
        ns0=vm((4 * HALO, LATENT), BF),
        ns1=vm((4 * HALO, PADDED), BF),
        nr1=vm((4 * HALO, PADDED), BF),
        ns2=vm((4 * HALO, LATENT), BF),
        mesh_ext=vm((NODES + 4 * HALO, LATENT), BF),
        ns3=vm((4 * HALO, LATENT), BF),
        nr3=vm((4 * HALO, LATENT), BF),
        near_sem=sems((4, 2)),
        far_sem=sems((4, 2, 2)),
        entered=pltpu.SemaphoreType.REGULAR,
        cot=vm((CHANNELS, GRID), BF),
        wn=vm((LATENT, LATENT), BF),
        ws=vm((2, LATENT, LATENT), BF),
        wr=vm((2, LATENT, LATENT), BF),
        wu=vm((2, LATENT, LATENT), BF),
        load_sem=sems((5,)),
        fars=[dict(source=vm((4 * FAR, 128), BF), target=vm((4 * FAR, 128), BF)) for _ in range(4)],
        groups=[
            dict(
                own=vm((NODES, width), F32),
                sc=vm((NODES, width), BF),
                rc=vm((NODES, width), BF),
                sx=vm((NODES, width), BF),
                rx=vm((192 if along else NODES, width), BF),
                fp=vm((width // 2 if along else width // 8, 128), F32),
                sp=vm((width // 2 if along else width // 8, 128), BF),
                rp=vm((width // 2 if along else 3 * width // 32, 128), BF),
                sem=sems((3, 2)),
            )
            for width, along in GROUPS
        ],
    )


def kernel(tree, xt, ct_far, we, wn_far, ws_far, wr_far, wu_far, dwt, el, es, ml, ms, dl, ds_, *rest):
    out_pred, out_embed, out_encode, out_source, out_target, out_refresh, out_decode = rest[:7]
    r = Refs(jax.tree.unflatten(tree, rest[7:]))
    for each, (width, along) in zip(r.groups, GROUPS):
        each.along = along
    g_u1, g_r1, g_su, g_r0, g_s0, g_en, g_de = r.groups
    b = lax.axis_index("lat")
    c = lax.axis_index("lon")
    me = b * SECTORS + c
    core = lax.rem(c, 2)
    place = c // 2

    barrier = pltpu.get_barrier_semaphore()

    def greet(t, carry):
        v = lax.rem(c + t, SECTORS)
        pl.semaphore_signal(barrier, inc=1, device_id=(b, v), device_id_type=MESH)
        return carry

    lax.fori_loop(1, SECTORS, greet, 0)

    def greet_bands(semaphore):
        for t in range(1, BANDS):
            u = lax.rem(b + t, BANDS)
            pl.semaphore_signal(semaphore, inc=1, device_id=(u, c), device_id_type=MESH)

    greet_bands(barrier)

    neighbours = (
        (b, lax.rem(c + SECTORS - 1, SECTORS)),
        (b, lax.rem(c + 1, SECTORS)),
        (lax.rem(b + BANDS - 1, BANDS), c),
        (lax.rem(b + 1, BANDS), c),
    )

    def drain(ref, sem):
        pltpu.make_async_copy(ref, ref, sem).wait()

    def near_start(i, source, target):
        for k in range(4):
            pltpu.make_async_remote_copy(
                source.at[pl.ds(k * HALO, HALO)],
                target.at[pl.ds((k ^ 1) * HALO, HALO)],
                r.near_sem.at[i, 0],
                r.near_sem.at[i, 1],
                device_id=neighbours[k],
                device_id_type=MESH,
            ).start()

    def near_wait(i, source, target):
        drain(target, r.near_sem.at[i, 1])
        drain(source, r.near_sem.at[i, 0])

    half = PEERS // 2
    deep, wide = c // 8, lax.rem(c // 2, 4)

    def peer(t, sign):
        w = half - 1 - lax.rem(t, half)
        u = lax.rem(b + BANDS + sign * lax.rem(w, 4), BANDS)
        z = lax.rem(deep + 4 + sign * lax.rem(w // 4, 4), 4)
        y = lax.rem(wide + 4 + sign * (w // 16), 4)
        return u, z * 8 + y * 2 + lax.rem(core + t // half, 2)

    def block(at):
        return pl.ds(pl.multiple_of(at * 16, 16), 16)

    def far_start(i, group, back):
        source, target = r.fars[i].source, r.fars[i].target

        def send(t, carry):
            u, v = peer(t, -1 if back else 1)
            there = u * SECTORS + v
            pltpu.make_async_remote_copy(
                source.at[block(t if back else there)],
                target.at[block(me if back else t)],
                r.far_sem.at[i, group, 0],
                r.far_sem.at[i, group, 1],
                device_id=(u, v),
                device_id_type=MESH,
            ).start()
            return carry

        if group == 0:
            lax.fori_loop(0, half - 1, send, 0)
            if back:
                target[block(me), :] = source[16 * (half - 1) : 16 * half, :]
            else:
                target[16 * (half - 1) : 16 * half, :] = source[block(me), :]
        else:
            lax.fori_loop(half, PEERS, send, 0)

    def far_wait(i, group):
        part = pl.ds(0, 16 * (half - 1 + group))
        drain(r.fars[i].target.at[part], r.far_sem.at[i, group, 1])
        drain(r.fars[i].source.at[part], r.far_sem.at[i, group, 0])

    packed = r.packed
    chunk = 32

    def pack(value, target, first=0):
        peers = value.shape[0] // SLOTS
        for i in range(SLOTS):
            for j in range(4):
                packed[pl.ds(first * 16 + 4 * j + i, peers, stride=16), :] = value[
                    i * peers : (i + 1) * peers, j * 128 : (j + 1) * 128
                ]
        rows = slice(first * 16, (first + peers) * 16)
        target[rows, :] = packed[rows, :].astype(BF)

    def unpack(source, first=0, peers=PEERS):
        rows = slice(first * 16, (first + peers) * 16)
        packed[rows, :] = source[rows, :].astype(F32)
        for i in range(SLOTS):
            at = first * SLOTS + i * peers
            for j in range(4):
                r.far[at : at + peers, j * 128 : (j + 1) * 128] = packed[
                    pl.ds(first * 16 + 4 * j + i, peers, stride=16), :
                ].astype(BF)

    def turned(g, value):
        order = 0 if g.along else 1
        return (
            mmt(r.p_own[order], value).astype(BF),
            mmt(r.p_oth[order], value).astype(BF),
        )

    def gradient(g, at, left, right):
        width = right.shape[1]
        sides = turned(g, left)
        g.own[:, at : at + width] = mm(sides[0], right)
        g.sc[:, at : at + width] = mm(sides[1], right).astype(BF)

    def core_start(g):
        pltpu.make_async_remote_copy(
            g.sc,
            g.rc,
            g.sem.at[0, 0],
            g.sem.at[0, 1],
            device_id=(b, c + 1 - 2 * core),
            device_id_type=MESH,
        ).start()

    def core_wait(g):
        drain(g.rc, g.sem.at[0, 1])
        drain(g.sc, g.sem.at[0, 0])
        total = g.own[...] + g.rc[...].astype(F32)
        g.own[...] = total
        g.sx[...] = total.astype(BF)

    def over_bands(g, hop, source, target, rows):
        for t in range(1, BANDS):
            u = lax.rem(b + t, BANDS)
            pltpu.make_async_remote_copy(
                source.at[pl.ds(pl.multiple_of(u * rows, 16), rows)],
                target.at[pl.ds((t - 1) * rows, rows)],
                g.sem.at[hop, 0],
                g.sem.at[hop, 1],
                device_id=(u, c),
                device_id_type=MESH,
            ).start()

    def over_plane(g, hop, source, target, rows):
        mine = pl.ds(pl.multiple_of(place * rows, 16), rows)

        def send(t, carry):
            q = lax.rem(place + t, 16)
            pltpu.make_async_remote_copy(
                source.at[pl.ds(pl.multiple_of(q * rows, 16), rows)],
                target.at[mine],
                g.sem.at[hop, 0],
                g.sem.at[hop, 1],
                device_id=(b, q * 2 + core),
                device_id_type=MESH,
            ).start()
            return carry

        lax.fori_loop(1, 16, send, 0)
        target[mine, :] = source[mine, :]

    def plane_sum(g, hop, source, target, rows):
        rest_of = pl.ds(0, 15 * rows)
        drain(target.at[rest_of], g.sem.at[hop, 1])
        drain(source.at[rest_of], g.sem.at[hop, 0])
        total = target[0:rows, :].astype(F32)
        for q in range(1, 16):
            total = total + target[q * rows : (q + 1) * rows, :].astype(F32)
        return total

    def band_sum(g, hop, source, target, rows, own):
        drain(target, g.sem.at[hop, 1])
        drain(source.at[pl.ds(0, 3 * rows)], g.sem.at[hop, 0])
        total = own[pl.ds(pl.multiple_of(b * rows, 8), rows), :]
        for t in range(3):
            total = total + target[t * rows : (t + 1) * rows, :].astype(F32)
        return total

    def first_start(g):
        core_wait(g)
        if g.along:
            over_bands(g, 1, g.sx, g.rx, 64)
        else:
            over_plane(g, 1, g.sx, g.rx, 16)

    def second_start(g):
        width = g.sc.shape[1]
        rows = width // 32
        if g.along:
            total = band_sum(g, 1, g.sx, g.rx, 64, g.own)
            for j in range(width // 128):
                for i in range(4):
                    g.fp[pl.ds(4 * j + i, 16, stride=rows), :] = total[
                        i * 16 : (i + 1) * 16, j * 128 : (j + 1) * 128
                    ]
        else:
            total = plane_sum(g, 1, g.sx, g.rx, 16)
            for u in range(4):
                for j in range(width // 128):
                    at = u * rows + 4 * j
                    g.fp[at : at + 4, :] = total[u * 4 : (u + 1) * 4, j * 128 : (j + 1) * 128]
        g.sp[...] = g.fp[...].astype(BF)
        if g.along:
            over_plane(g, 2, g.sp, g.rp, rows)
        else:
            over_bands(g, 2, g.sp, g.rp, rows)

    def finish(g):
        rows = g.sc.shape[1] // 32
        if g.along:
            return plane_sum(g, 2, g.sp, g.rp, rows)
        return band_sum(g, 2, g.sp, g.rp, rows, g.fp)

    def deliver(total, at, write):
        for j in range(4):
            row = 4 * (at // 128 + j)
            write(j, total[row : row + 4, :])

    wn, ws, wr, wu = r.wn, r.ws, r.wr, r.wu
    loads = [
        pltpu.make_async_copy(source, target, r.load_sem.at[i])
        for i, (source, target) in enumerate(
            ((wn_far, wn), (ws_far, ws), (wr_far, wr), (wu_far, wu), (ct_far, r.cot))
        )
    ]
    for each in loads:
        each.start()

    for target, source in ((r.xp, xt), (r.wep, we), (r.dwp, dwt)):
        target[224:256, :] = jnp.zeros((32, source.shape[1]), BF)
        target[0:CHANNELS, :] = source[...]

    def embed(i, carry):
        rows = pl.ds(pl.multiple_of(i * 256, 256), 256)
        inner = tmm(r.xp[:, rows], r.wep[...])
        s = sigmoid(inner)
        value = inner * s
        r.grid_ext[rows, :] = value.astype(BF)
        r.gslope[rows, :] = (s + value * (1.0 - s)).astype(BF)
        return carry

    lax.fori_loop(0, 4, embed, 0)

    def near_row(lists):
        return jnp.concatenate([lists[k : k + 1, :] for k in range(4)], axis=1)

    encode_row = near_row(el)
    decode_row = near_row(dl)
    encode_pick = hot(column(encode_row) == iota((4 * HALO, GRID), 1))
    r.ns0[...] = mm(encode_pick, r.grid_ext[0:GRID, :]).astype(BF)

    pl.semaphore_wait(barrier, SECTORS - 1 + BANDS - 1)
    greet_bands(r.entered)
    halo_grid = r.grid_ext.at[pl.ds(GRID, 4 * HALO)]
    near_start(0, r.ns0, halo_grid)
    for each in loads:
        each.wait()
    r.cp[224:256, :] = jnp.zeros((32, GRID), BF)
    r.cp[0:CHANNELS, :] = r.cot[...]

    es_col = jnp.transpose(es[...])
    for part in range(5):
        where = iota((NODES, 256), 1) + part * 256
        total = jnp.zeros((NODES, 256), F32)
        for k in range(DEGREE):
            total = total + jnp.where(es_col[:, k : k + 1] == where, 1.0, 0.0)
        r.enc_c[:, part * 256 : (part + 1) * 256] = total.astype(BF)
    encode_local = mm(r.enc_c[:, 0:GRID], r.grid_ext[0:GRID, :])

    for i in range(SLOTS):
        row = ml[i : i + 1, :]
        r.list_r[i * PEERS : (i + 1) * PEERS, :] = hot(column(row) == iota((PEERS, NODES), 1))

    near_wait(0, r.ns0, halo_grid)
    encode_input = (encode_local + mm(r.enc_c[:, GRID:], r.grid_ext[GRID:, :])).astype(BF)
    r.enc_in[...] = encode_input
    encode_inner = mm(encode_input, wn[...])
    s = sigmoid(encode_inner)
    value = encode_inner * s
    r.mesh[0] = value.astype(BF)
    r.enc_slope[...] = s + value * (1.0 - s)

    def send_rows(layer):
        sender = mm(r.mesh[layer], ws[layer]).astype(BF)
        pack(mm(r.list_r[...], sender), r.fars[layer].source)
        far_start(layer, 0, False)
        far_start(layer, 1, False)
        return sender

    def local_rows(layer, sender):
        receiver = mm(r.mesh[layer], wr[layer])
        for k in range(DEGREE):
            rows = slice(k * NODES, (k + 1) * NODES)
            r.base[layer, rows, :] = mm(r.oh_loc[rows, :], sender) + receiver

    def far_rows(layer, edge):
        far_wait(layer, 0)
        unpack(r.fars[layer].target, 0, half)

        def first(k, carry):
            rows = pl.ds(pl.multiple_of(k * NODES, NODES), NODES)
            r.base[layer, rows, :] += mm(r.oh_far[rows, 0 : FAR // 2], r.far[0 : FAR // 2, :])
            return carry

        lax.fori_loop(0, DEGREE, first, 0)
        far_wait(layer, 1)
        unpack(r.fars[layer].target, half, half)
        r.total[...] = jnp.zeros((NODES, LATENT), F32)

        def add(k, carry):
            at = pl.multiple_of(k * NODES, NODES)
            rows = pl.ds(at, NODES)
            far = mm(r.oh_far[rows, FAR // 2 :], r.far[FAR // 2 :, :])
            for h in range(NODES // chunk):
                part = slice(h * chunk, (h + 1) * chunk)
                rows = pl.ds(at + h * chunk, chunk)
                inner = r.base[layer, rows, :] + far[part, :]
                s = sigmoid(inner)
                value = inner * s
                r.total[part, :] += value
                edge(inner, s, value, part, rows)
            return carry

        lax.fori_loop(0, DEGREE, add, 0)
        r.agg[layer] = r.total[...].astype(BF)

    pl.semaphore_wait(r.entered, BANDS - 1)
    sender = send_rows(0)

    def far_index(v):
        k = v - NODES
        p = k >> 2
        w = ((b - (p >> 5)) & 3) + 4 * ((deep - (p >> 3)) & 3) + 16 * ((wide - (p >> 1)) & 3)
        group = (core - p) & 1
        return jnp.where(k >= 0, group * (FAR // 2) + (k & 3) * half + half - 1 - w, -1)

    ms_row = ms[...]
    ms_col = jnp.transpose(ms_row)
    far_row = far_index(ms_row)
    far_col = far_index(ms_col)
    for k in range(DEGREE):
        rows = slice(k * NODES, (k + 1) * NODES)
        r.oh_loc[rows, :] = hot(ms_col[:, k : k + 1] == iota((NODES, NODES), 1))
        r.oh_far[rows, :] = hot(far_col[:, k : k + 1] == iota((NODES, FAR), 1))
    local_rows(0, sender)

    for part in range(2):
        where = iota((NODES, GRID), 0) + part * NODES
        total = jnp.zeros((NODES, GRID), F32)
        for k in range(3):
            total = total + jnp.where(ds_[k : k + 1, :] == where, 1.0, 0.0)
        r.dec_t[part * NODES : (part + 1) * NODES, :] = total.astype(BF)
    r.ns1[...] = mmt(r.dec_t[NODES:, :], r.cp[...]).astype(BF)
    near_start(1, r.ns1, r.nr1)
    r.dext[...] = mmt(r.dec_t[0:NODES, :], r.cp[...])

    def keep(inner, s, value, part, rows):
        r.base[0, rows, :] = inner

    far_rows(0, keep)
    r.mesh[1] = (r.mesh[0].astype(F32) + mm(r.agg[0], wu[0])).astype(BF)

    sender = send_rows(1)
    local_rows(1, sender)

    decode_spread = hot(decode_row == iota((NODES, 4 * HALO), 0))
    near_wait(1, r.ns1, r.nr1)
    decode_back = (r.dext[...] + mm(decode_spread, r.nr1[...])).astype(BF)
    r.dback[...] = decode_back
    latent_back = mm(decode_back, r.dwp[...])
    r.lat[...] = latent_back
    out_back = latent_back.astype(BF)
    r.ob[...] = out_back
    r.ab[...] = mmt(out_back, wu[1])

    def slopes(i, carry):
        rows = pl.ds(pl.multiple_of(i * 64, 64), 64)
        inner = r.base[0, rows, :]
        s = sigmoid(inner)
        r.slope[rows, :] = (s + inner * s * (1.0 - s)).astype(BF)
        return carry

    lax.fori_loop(0, EDGES // 64, slopes, 0)
    for k in range(DEGREE):
        rows = slice(k * NODES, (k + 1) * NODES)
        r.t_loc[:, rows] = hot(ms_row[k : k + 1, :] == iota((NODES, NODES), 0))
        r.t_far[:, rows] = hot(far_row[k : k + 1, :] == iota((FAR, NODES), 0))
    for i in range(SLOTS):
        row = ml[i : i + 1, :]
        r.list_t[:, i * PEERS : (i + 1) * PEERS] = hot(row == iota((NODES, PEERS), 0))

    index = iota((NODES, LATENT), 0)
    named = iota((NODES, LATENT), 1)
    by_band = (index // 64) * 128 + (index % 16) * 8 + (index // 16) % 4
    by_place = (index // 16) * 8 + ((index // 4) % 4) * 128 + index % 4
    for order, first in enumerate((by_band, by_place)):
        r.p_own[order] = hot(first + core * 4 == named)
        r.p_oth[order] = hot(first + (1 - core) * 4 == named)

    r.back[...] = jnp.zeros((NODES, LATENT), F32)

    def turn(inner, s, value, part, rows):
        back = r.ab[part, :] * (s + value * (1.0 - s))
        r.back[part, :] += back
        r.ib[rows, :] = back.astype(BF)

    far_rows(1, turn)
    r.rb[...] = r.back[...].astype(BF)

    def edges_back(i, carry):
        at = pl.multiple_of(i * chunk, chunk)
        back = jnp.zeros((chunk, LATENT), F32)
        given = r.ab[pl.ds(at, chunk), :]
        for k in range(DEGREE):
            rows = pl.ds(k * NODES + at, chunk)
            edge = given * r.slope[rows, :].astype(F32)
            back = back + edge
            r.ib[rows, :] = edge.astype(BF)
        r.rb[pl.ds(at, chunk), :] = back.astype(BF)
        return carry

    def return_start(slot):
        for group in range(2):
            rows = slice(group * (FAR // 2), (group + 1) * (FAR // 2))
            pack(mm(r.t_far[rows, :], r.ib[...]), r.fars[slot].source, group * half)
            far_start(slot, group, True)

    def return_local(layer):
        r.sback[...] = mm(r.t_loc[...], r.ib[...])
        r.lat[...] += mmt(r.rb[...], wr[layer])

    def return_end(slot, layer):
        unpack(r.fars[slot].target)
        sender_b = (r.sback[...] + mm(r.list_t[...], r.far[...])).astype(BF)
        r.lat[...] += mmt(sender_b, ws[layer])
        return sender_b

    return_start(2)
    mesh_last = (r.mesh[1].astype(F32) + mm(r.agg[1], wu[1])).astype(BF)
    r.mesh[2] = mesh_last
    r.mesh_ext[0:NODES, :] = mesh_last
    decode_pick = hot(column(decode_row) == iota((4 * HALO, NODES), 1))
    r.ns2[...] = mm(decode_pick, mesh_last).astype(BF)
    halo_mesh = r.mesh_ext.at[pl.ds(NODES, 4 * HALO)]
    near_start(2, r.ns2, halo_mesh)
    return_local(1)
    gradient(g_u1, 0, r.ob[...], r.agg[1])
    core_start(g_u1)
    gradient(g_r1, 0, r.rb[...], r.mesh[1])
    core_start(g_r1)
    gradient(g_de, 0, mesh_last, r.dback[...])
    for part in range(5):
        where_t = iota((256, NODES), 0) + part * 256
        total_t = jnp.zeros((256, NODES), F32)
        for k in range(DEGREE):
            total_t = total_t + jnp.where(es[k : k + 1, :] == where_t, 1.0, 0.0)
        r.enc_t[part * 256 : (part + 1) * 256, :] = total_t.astype(BF)
    first_start(g_u1)
    first_start(g_r1)
    far_wait(2, 0)
    far_wait(2, 1)
    sender_b1 = return_end(2, 1)

    out_back = r.lat[...].astype(BF)
    r.ob[...] = out_back
    r.ab[...] = mmt(out_back, wu[0])
    lax.fori_loop(0, NODES // chunk, edges_back, 0)
    return_start(3)
    return_local(0)
    gradient(g_su, 0, sender_b1, r.mesh[1])
    gradient(g_su, 512, r.ob[...], r.agg[0])
    core_start(g_su)
    gradient(g_r0, 0, r.rb[...], r.mesh[0])
    core_start(g_r0)
    near_wait(2, r.ns2, halo_mesh)
    decoded = mmt(r.dwp[...], r.mesh_ext[...]).astype(BF)
    forecast = r.xp[...].astype(F32) + mm(decoded, r.dec_t[...])
    out_pred[...] = forecast[0:CHANNELS, :].astype(BF)
    first_start(g_su)
    first_start(g_r0)
    second_start(g_u1)
    second_start(g_r1)
    far_wait(3, 0)
    far_wait(3, 1)
    sender_b0 = return_end(3, 0)

    encode_back = (r.lat[...] * r.enc_slope[...]).astype(BF)
    input_back = mmt(encode_back, wn[...]).astype(BF)
    r.ns3[...] = mm(r.enc_t[GRID:, :], input_back).astype(BF)
    near_start(3, r.ns3, r.nr3)
    gradient(g_s0, 0, sender_b0, r.mesh[0])
    core_start(g_s0)
    gradient(g_en, 0, encode_back, r.enc_in[...])
    core_start(g_en)
    r.gback[...] = mm(r.enc_t[0:GRID, :], input_back)
    encode_spread = hot(encode_row == iota((GRID, 4 * HALO), 0))
    first_start(g_s0)
    first_start(g_en)
    second_start(g_su)
    second_start(g_r0)
    near_wait(3, r.ns3, r.nr3)
    r.gback[...] += mm(encode_spread, r.nr3[...])
    r.eb[...] = (r.gback[...] * r.gslope[...].astype(F32)).astype(BF)
    across = mm(r.xp[...], r.eb[...]).astype(BF)
    g_de.own[:, 256:512] = mmt(r.p_own[0], across)
    g_de.sc[:, 256:512] = mmt(r.p_oth[0], across).astype(BF)
    core_start(g_de)

    def into(ref, layer=None):
        def write(j, value):
            if layer is None:
                ref[:, j * 128 : (j + 1) * 128] = value
            else:
                ref[layer, :, j * 128 : (j + 1) * 128] = value

        return write

    first_start(g_de)
    second_start(g_s0)
    second_start(g_en)
    deliver(finish(g_u1), 0, into(out_refresh, 1))
    deliver(finish(g_r1), 0, into(out_target, 1))
    second_start(g_de)
    total = finish(g_su)
    deliver(total, 0, into(out_source, 1))
    deliver(total, 512, into(out_refresh, 0))
    deliver(finish(g_r0), 0, into(out_target, 0))
    deliver(finish(g_s0), 0, into(out_source, 0))
    deliver(finish(g_en), 0, into(out_encode))
    total = finish(g_de)
    for ref, row in ((out_decode, 0), (out_embed, 8)):
        ref[:, 0:128] = total[row : row + 4, :]
        ref[:, 128:CHANNELS] = total[row + 4 : row + 8, 0 : CHANNELS - 128]


def hand_over(*refs):
    for source, target in zip(refs[:7], refs[7:]):
        target[...] = source[...]


def on_device(
    lattice_feature_values,
    cotangent,
    embed_weight,
    encode_weight,
    sender_weight,
    receiver_weight,
    update_weight,
    decode_weight,
    encode_lists,
    encode_sources,
    mesh_lists,
    mesh_sources,
    decode_lists,
    decoder_edge_sources,
):
    spec, tree = jax.tree.flatten(scratch())
    whole = pl.BlockSpec(memory_space=pltpu.VMEM)
    far = pl.BlockSpec(memory_space=pl.ANY)
    shape = jax.ShapeDtypeStruct
    shapes = (
        shape((CHANNELS, GRID), BF),
        shape((4, CHANNELS), F32),
        shape((4, LATENT), F32),
        shape((2, 4, LATENT), F32),
        shape((2, 4, LATENT), F32),
        shape((2, 4, LATENT), F32),
        shape((4, CHANNELS), F32),
    )
    outs = pl.pallas_call(
        functools.partial(kernel, tree),
        out_shape=shapes,
        in_specs=[whole, far, whole, far, far, far, far] + [whole] * 7,
        out_specs=(whole,) * 7,
        scratch_shapes=spec,
        compiler_params=pltpu.CompilerParams(
            collective_id=0, has_side_effects=True, vmem_limit_bytes=60 * 1024 * 1024
        ),
    )(
        lattice_feature_values.T,
        cotangent.T,
        embed_weight,
        encode_weight,
        sender_weight,
        receiver_weight,
        update_weight,
        decode_weight.T,
        encode_lists,
        encode_sources.T,
        mesh_lists.T,
        mesh_sources.T,
        decode_lists,
        decoder_edge_sources.T,
    )
    outs = pl.pallas_call(
        hand_over,
        out_shape=shapes,
        in_specs=[whole] * 7,
        out_specs=(whole,) * 7,
    )(*outs)
    return (
        outs[0].T,
        outs[1].T,
        outs[2].T,
        outs[3].transpose(0, 2, 1),
        outs[4].transpose(0, 2, 1),
        outs[5].transpose(0, 2, 1),
        outs[6],
    )


def solution(mesh):
    return jax.shard_map(
        on_device,
        mesh=mesh,
        in_specs=(
            P(("lat", "lon"), None),
            P(("lat", "lon"), None),
            P(),
            P(),
            P(),
            P(),
            P(),
            P(),
            P(("lat", "lon"), None),
            P(("lat", "lon"), None),
            P(("lat", "lon"), None),
            P(("lat", "lon"), None),
            P(("lat", "lon"), None),
            P(("lat", "lon"), None),
        ),
        out_specs=(
            P(("lat", "lon"), None),
            P(None, ("lat", "lon")),
            P(None, ("lat", "lon")),
            P(None, None, ("lat", "lon")),
            P(None, None, ("lat", "lon")),
            P(None, None, ("lat", "lon")),
            P(("lat", "lon"), None),
        ),
        check_vma=False,
    )
```

```python
import functools

import jax
import jax.numpy as jnp
from jax import lax
from jax.experimental import pallas as pl
from jax.experimental.pallas import tpu as pltpu
from jax.sharding import PartitionSpec as P

BF = jnp.bfloat16
F32 = jnp.float32
MESH = pl.DeviceIdType.MESH

BANDS, SECTORS, PEERS = 4, 32, 128
LATENT, CHANNELS, PADDED = 512, 227, 256
GRID, NODES, HALO, SLOTS, DEGREE = 1024, 256, 64, 4, 8
EDGES = NODES * DEGREE
FAR = PEERS * SLOTS


def mm(a, b):
    return lax.dot_general(a, b, (((1,), (0,)), ((), ())), preferred_element_type=F32)


def mmt(a, b):
    return lax.dot_general(a, b, (((1,), (1,)), ((), ())), preferred_element_type=F32)


def tmm(a, b):
    return lax.dot_general(a, b, (((0,), (0,)), ((), ())), preferred_element_type=F32)


def sigmoid(v):
    return 0.5 * jnp.tanh(0.5 * v) + 0.5


def iota(shape, dim):
    return lax.broadcasted_iota(jnp.int32, shape, dim)


def hot(mask):
    return jnp.where(mask, 1.0, 0.0).astype(BF)


def column(row):
    return jnp.transpose(jnp.broadcast_to(row, (8, row.shape[1])))[:, :1]


class Refs:
    def __init__(self, named):
        for name, ref in named.items():
            if isinstance(ref, list):
                ref = [Refs(each) for each in ref]
            setattr(self, name, ref)


GROUPS = (
    (512, True),
    (512, False),
    (256, True),
    (1024, True),
    (512, False),
    (1024, False),
    (256, True),
)


def scratch():
    vm = pltpu.VMEM
    sems = pltpu.SemaphoreType.DMA
    return dict(
        xp=vm((PADDED, GRID), BF),
        cp=vm((PADDED, GRID), BF),
        wep=vm((PADDED, LATENT), BF),
        dwp=vm((PADDED, LATENT), BF),
        grid_ext=vm((GRID + 4 * HALO, LATENT), BF),
        gslope=vm((GRID, LATENT), BF),
        enc_c=vm((NODES, GRID + 4 * HALO), BF),
        enc_t=vm((GRID + 4 * HALO, NODES), BF),
        dec_t=vm((NODES + 4 * HALO, GRID), BF),
        oh_loc=vm((EDGES, NODES), BF),
        oh_far=vm((EDGES, FAR), BF),
        t_loc=vm((NODES, EDGES), BF),
        t_far=vm((FAR, EDGES), BF),
        list_r=vm((FAR, NODES), BF),
        list_t=vm((NODES, FAR), BF),
        p_own=vm((2, NODES, LATENT), BF),
        p_oth=vm((2, NODES, LATENT), BF),
        enc_in=vm((NODES, LATENT), BF),
        enc_slope=vm((NODES, LATENT), F32),
        mesh=vm((3, NODES, LATENT), BF),
        agg=vm((2, NODES, LATENT), BF),
        base=vm((2, EDGES, LATENT), F32),
        slope=vm((EDGES, LATENT), BF),
        ib=vm((EDGES, LATENT), BF),
        rb=vm((NODES, LATENT), BF),
        back=vm((NODES, LATENT), F32),
        total=vm((NODES, LATENT), F32),
        ab=vm((NODES, LATENT), F32),
        ob=vm((NODES, LATENT), BF),
        lat=vm((NODES, LATENT), F32),
        dback=vm((NODES, PADDED), BF),
        dext=vm((NODES, PADDED), F32),
        sback=vm((NODES, LATENT), F32),
        gback=vm((GRID, LATENT), F32),
        eb=vm((GRID, LATENT), BF),
        far=vm((FAR, LATENT), BF),
        packed=vm((4 * FAR, 128), F32),
        ns0=vm((4 * HALO, LATENT), BF),
        ns1=vm((4 * HALO, PADDED), BF),
        nr1=vm((4 * HALO, PADDED), BF),
        ns2=vm((4 * HALO, LATENT), BF),
        mesh_ext=vm((NODES + 4 * HALO, LATENT), BF),
        ns3=vm((4 * HALO, LATENT), BF),
        nr3=vm((4 * HALO, LATENT), BF),
        near_sem=sems((4, 2)),
        far_sem=sems((4, 2, 2)),
        entered=pltpu.SemaphoreType.REGULAR,
        cot=vm((CHANNELS, GRID), BF),
        wn=vm((LATENT, LATENT), BF),
        ws=vm((2, LATENT, LATENT), BF),
        wr=vm((2, LATENT, LATENT), BF),
        wu=vm((2, LATENT, LATENT), BF),
        load_sem=sems((5,)),
        fars=[dict(source=vm((4 * FAR, 128), BF), target=vm((4 * FAR, 128), BF)) for _ in range(4)],
        groups=[
            dict(
                own=vm((NODES, width), F32),
                sc=vm((NODES, width), BF),
                rc=vm((NODES, width), BF),
                sx=vm((NODES, width), BF),
                rx=vm((192 if along else NODES, width), BF),
                fp=vm((width // 2 if along else width // 8, 128), F32),
                sp=vm((width // 2 if along else width // 8, 128), BF if width > 256 else F32),
                rp=vm((width // 2 if along else 3 * width // 32, 128), BF if width > 256 else F32),
                sem=sems((3, 2)),
            )
            for width, along in GROUPS
        ],
    )


def kernel(tree, xt, ct_far, we, wn_far, ws_far, wr_far, wu_far, dwt, el, es, ml, ms, dl, ds_, *rest):
    out_pred, out_embed, out_encode, out_source, out_target, out_refresh, out_decode = rest[:7]
    r = Refs(jax.tree.unflatten(tree, rest[7:]))
    for each, (width, along) in zip(r.groups, GROUPS):
        each.along = along
    g_u1, g_r1, g_dc, g_su, g_r0, g_se, g_em = r.groups
    b = lax.axis_index("lat")
    c = lax.axis_index("lon")
    me = b * SECTORS + c
    core = lax.rem(c, 2)
    place = c // 2

    barrier = pltpu.get_barrier_semaphore()

    def greet(t, carry):
        v = lax.rem(c + t, SECTORS)
        pl.semaphore_signal(barrier, inc=1, device_id=(b, v), device_id_type=MESH)
        return carry

    lax.fori_loop(1, SECTORS, greet, 0)

    def greet_bands(semaphore):
        for t in range(1, BANDS):
            u = lax.rem(b + t, BANDS)
            pl.semaphore_signal(semaphore, inc=1, device_id=(u, c), device_id_type=MESH)

    greet_bands(barrier)

    neighbours = (
        (b, lax.rem(c + SECTORS - 1, SECTORS)),
        (b, lax.rem(c + 1, SECTORS)),
        (lax.rem(b + BANDS - 1, BANDS), c),
        (lax.rem(b + 1, BANDS), c),
    )

    def drain(ref, sem):
        pltpu.make_async_copy(ref, ref, sem).wait()

    def near_start(i, source, target):
        for k in range(4):
            pltpu.make_async_remote_copy(
                source.at[pl.ds(k * HALO, HALO)],
                target.at[pl.ds((k ^ 1) * HALO, HALO)],
                r.near_sem.at[i, 0],
                r.near_sem.at[i, 1],
                device_id=neighbours[k],
                device_id_type=MESH,
            ).start()

    def near_wait(i, source, target):
        drain(target, r.near_sem.at[i, 1])
        drain(source, r.near_sem.at[i, 0])

    half = PEERS // 2
    deep, wide = c // 8, lax.rem(c // 2, 4)

    def peer(t, sign):
        w = half - 1 - lax.rem(t, half)
        u = lax.rem(b + BANDS + sign * lax.rem(w, 4), BANDS)
        z = lax.rem(deep + 4 + sign * lax.rem(w // 4, 4), 4)
        y = lax.rem(wide + 4 + sign * (w // 16), 4)
        return u, z * 8 + y * 2 + lax.rem(core + t // half, 2)

    def block(at):
        return pl.ds(pl.multiple_of(at * 16, 16), 16)

    def far_start(i, group, back):
        source, target = r.fars[i].source, r.fars[i].target

        def send(t, carry):
            u, v = peer(t, -1 if back else 1)
            there = u * SECTORS + v
            pltpu.make_async_remote_copy(
                source.at[block(t if back else there)],
                target.at[block(me if back else t)],
                r.far_sem.at[i, group, 0],
                r.far_sem.at[i, group, 1],
                device_id=(u, v),
                device_id_type=MESH,
            ).start()
            return carry

        if group == 0:
            lax.fori_loop(0, half - 1, send, 0)
            if back:
                target[block(me), :] = source[16 * (half - 1) : 16 * half, :]
            else:
                target[16 * (half - 1) : 16 * half, :] = source[block(me), :]
        else:
            lax.fori_loop(half, PEERS, send, 0)

    def far_wait(i, group):
        part = pl.ds(0, 16 * (half - 1 + group))
        drain(r.fars[i].target.at[part], r.far_sem.at[i, group, 1])
        drain(r.fars[i].source.at[part], r.far_sem.at[i, group, 0])

    packed = r.packed
    chunk = 32

    def pack(value, target, first=0):
        peers = value.shape[0] // SLOTS
        for i in range(SLOTS):
            for j in range(4):
                packed[pl.ds(first * 16 + 4 * j + i, peers, stride=16), :] = value[
                    i * peers : (i + 1) * peers, j * 128 : (j + 1) * 128
                ]
        rows = slice(first * 16, (first + peers) * 16)
        target[rows, :] = packed[rows, :].astype(BF)

    def unpack(source, first=0, peers=PEERS):
        rows = slice(first * 16, (first + peers) * 16)
        packed[rows, :] = source[rows, :].astype(F32)
        for i in range(SLOTS):
            at = first * SLOTS + i * peers
            for j in range(4):
                r.far[at : at + peers, j * 128 : (j + 1) * 128] = packed[
                    pl.ds(first * 16 + 4 * j + i, peers, stride=16), :
                ].astype(BF)

    def turned(g, value):
        order = 0 if g.along else 1
        return (
            mmt(r.p_own[order], value).astype(BF),
            mmt(r.p_oth[order], value).astype(BF),
        )

    def gradient(g, at, left, right):
        width = right.shape[1]
        sides = turned(g, left)
        g.own[:, at : at + width] = mm(sides[0], right)
        g.sc[:, at : at + width] = mm(sides[1], right).astype(BF)

    def core_start(g):
        pltpu.make_async_remote_copy(
            g.sc,
            g.rc,
            g.sem.at[0, 0],
            g.sem.at[0, 1],
            device_id=(b, c + 1 - 2 * core),
            device_id_type=MESH,
        ).start()

    def core_wait(g):
        drain(g.rc, g.sem.at[0, 1])
        drain(g.sc, g.sem.at[0, 0])
        total = g.own[...] + g.rc[...].astype(F32)
        g.own[...] = total
        g.sx[...] = total.astype(BF)

    def over_bands(g, hop, source, target, rows):
        for t in range(1, BANDS):
            u = lax.rem(b + t, BANDS)
            pltpu.make_async_remote_copy(
                source.at[pl.ds(pl.multiple_of(u * rows, 16), rows)],
                target.at[pl.ds((t - 1) * rows, rows)],
                g.sem.at[hop, 0],
                g.sem.at[hop, 1],
                device_id=(u, c),
                device_id_type=MESH,
            ).start()

    def over_plane(g, hop, source, target, rows):
        mine = pl.ds(pl.multiple_of(place * rows, min(rows, 16)), rows)

        def send(t, carry):
            q = lax.rem(place + t, 16)
            pltpu.make_async_remote_copy(
                source.at[pl.ds(pl.multiple_of(q * rows, min(rows, 16)), rows)],
                target.at[mine],
                g.sem.at[hop, 0],
                g.sem.at[hop, 1],
                device_id=(b, q * 2 + core),
                device_id_type=MESH,
            ).start()
            return carry

        lax.fori_loop(1, 16, send, 0)
        target[mine, :] = source[mine, :]

    def plane_sum(g, hop, source, target, rows):
        rest_of = pl.ds(0, 15 * rows)
        drain(target.at[rest_of], g.sem.at[hop, 1])
        drain(source.at[rest_of], g.sem.at[hop, 0])
        total = target[0:rows, :].astype(F32)
        for q in range(1, 16):
            total = total + target[q * rows : (q + 1) * rows, :].astype(F32)
        return total

    def band_sum(g, hop, source, target, rows, own):
        drain(target, g.sem.at[hop, 1])
        drain(source.at[pl.ds(0, 3 * rows)], g.sem.at[hop, 0])
        total = own[pl.ds(pl.multiple_of(b * rows, 8), rows), :]
        for t in range(3):
            total = total + target[t * rows : (t + 1) * rows, :].astype(F32)
        return total

    def first_start(g):
        core_wait(g)
        if g.along:
            over_bands(g, 1, g.sx, g.rx, 64)
        else:
            over_plane(g, 1, g.sx, g.rx, 16)

    def second_start(g):
        width = g.sc.shape[1]
        rows = width // 32
        if g.along:
            total = band_sum(g, 1, g.sx, g.rx, 64, g.own)
            for j in range(width // 128):
                for i in range(4):
                    g.fp[pl.ds(4 * j + i, 16, stride=rows), :] = total[
                        i * 16 : (i + 1) * 16, j * 128 : (j + 1) * 128
                    ]
        else:
            total = plane_sum(g, 1, g.sx, g.rx, 16)
            for u in range(4):
                for j in range(width // 128):
                    at = u * rows + 4 * j
                    g.fp[at : at + 4, :] = total[u * 4 : (u + 1) * 4, j * 128 : (j + 1) * 128]
        g.sp[...] = g.fp[...].astype(g.sp.dtype)
        if g.along:
            over_plane(g, 2, g.sp, g.rp, rows)
        else:
            over_bands(g, 2, g.sp, g.rp, rows)

    def finish(g):
        rows = g.sc.shape[1] // 32
        if g.along:
            return plane_sum(g, 2, g.sp, g.rp, rows)
        return band_sum(g, 2, g.sp, g.rp, rows, g.fp)

    def deliver(total, at, write):
        for j in range(4):
            row = 4 * (at // 128 + j)
            write(j, total[row : row + 4, :])

    wn, ws, wr, wu = r.wn, r.ws, r.wr, r.wu
    loads = [
        pltpu.make_async_copy(source, target, r.load_sem.at[i])
        for i, (source, target) in enumerate(
            ((wn_far, wn), (ws_far, ws), (wr_far, wr), (wu_far, wu), (ct_far, r.cot))
        )
    ]
    for each in loads:
        each.start()

    for target, source in ((r.xp, xt), (r.wep, we), (r.dwp, dwt)):
        target[224:256, :] = jnp.zeros((32, source.shape[1]), BF)
        target[0:CHANNELS, :] = source[...]

    def embed(i, carry):
        rows = pl.ds(pl.multiple_of(i * 256, 256), 256)
        inner = tmm(r.xp[:, rows], r.wep[...])
        s = sigmoid(inner)
        value = inner * s
        r.grid_ext[rows, :] = value.astype(BF)
        r.gslope[rows, :] = (s + value * (1.0 - s)).astype(BF)
        return carry

    lax.fori_loop(0, 4, embed, 0)

    def near_row(lists):
        return jnp.concatenate([lists[k : k + 1, :] for k in range(4)], axis=1)

    encode_row = near_row(el)
    decode_row = near_row(dl)
    encode_pick = hot(column(encode_row) == iota((4 * HALO, GRID), 1))
    r.ns0[...] = mm(encode_pick, r.grid_ext[0:GRID, :]).astype(BF)

    pl.semaphore_wait(barrier, SECTORS - 1 + BANDS - 1)
    greet_bands(r.entered)
    halo_grid = r.grid_ext.at[pl.ds(GRID, 4 * HALO)]
    near_start(0, r.ns0, halo_grid)
    for each in loads:
        each.wait()
    r.cp[224:256, :] = jnp.zeros((32, GRID), BF)
    r.cp[0:CHANNELS, :] = r.cot[...]

    es_col = jnp.transpose(es[...])
    for part in range(5):
        where = iota((NODES, 256), 1) + part * 256
        total = jnp.zeros((NODES, 256), F32)
        for k in range(DEGREE):
            total = total + jnp.where(es_col[:, k : k + 1] == where, 1.0, 0.0)
        r.enc_c[:, part * 256 : (part + 1) * 256] = total.astype(BF)
    encode_local = mm(r.enc_c[:, 0:GRID], r.grid_ext[0:GRID, :])

    for i in range(SLOTS):
        row = ml[i : i + 1, :]
        r.list_r[i * PEERS : (i + 1) * PEERS, :] = hot(column(row) == iota((PEERS, NODES), 1))

    near_wait(0, r.ns0, halo_grid)
    encode_input = (encode_local + mm(r.enc_c[:, GRID:], r.grid_ext[GRID:, :])).astype(BF)
    r.enc_in[...] = encode_input
    encode_inner = mm(encode_input, wn[...])
    s = sigmoid(encode_inner)
    value = encode_inner * s
    r.mesh[0] = value.astype(BF)
    r.enc_slope[...] = s + value * (1.0 - s)

    def send_rows(layer):
        sender = mm(r.mesh[layer], ws[layer]).astype(BF)
        pack(mm(r.list_r[...], sender), r.fars[layer].source)
        far_start(layer, 0, False)
        far_start(layer, 1, False)
        return sender

    def local_rows(layer, sender):
        receiver = mm(r.mesh[layer], wr[layer])
        for k in range(DEGREE):
            rows = slice(k * NODES, (k + 1) * NODES)
            r.base[layer, rows, :] = mm(r.oh_loc[rows, :], sender) + receiver

    def far_rows(layer, edge):
        far_wait(layer, 0)
        unpack(r.fars[layer].target, 0, half)

        def first(k, carry):
            rows = pl.ds(pl.multiple_of(k * NODES, NODES), NODES)
            r.base[layer, rows, :] += mm(r.oh_far[rows, 0 : FAR // 2], r.far[0 : FAR // 2, :])
            return carry

        lax.fori_loop(0, DEGREE, first, 0)
        far_wait(layer, 1)
        unpack(r.fars[layer].target, half, half)
        r.total[...] = jnp.zeros((NODES, LATENT), F32)

        def add(k, carry):
            at = pl.multiple_of(k * NODES, NODES)
            rows = pl.ds(at, NODES)
            far = mm(r.oh_far[rows, FAR // 2 :], r.far[FAR // 2 :, :])
            for h in range(NODES // chunk):
                part = slice(h * chunk, (h + 1) * chunk)
                rows = pl.ds(at + h * chunk, chunk)
                inner = r.base[layer, rows, :] + far[part, :]
                s = sigmoid(inner)
                value = inner * s
                r.total[part, :] += value
                edge(inner, s, value, part, rows)
            return carry

        lax.fori_loop(0, DEGREE, add, 0)
        r.agg[layer] = r.total[...].astype(BF)

    pl.semaphore_wait(r.entered, BANDS - 1)
    sender = send_rows(0)

    def far_index(v):
        k = v - NODES
        p = k >> 2
        w = ((b - (p >> 5)) & 3) + 4 * ((deep - (p >> 3)) & 3) + 16 * ((wide - (p >> 1)) & 3)
        group = (core - p) & 1
        return jnp.where(k >= 0, group * (FAR // 2) + (k & 3) * half + half - 1 - w, -1)

    ms_row = ms[...]
    ms_col = jnp.transpose(ms_row)
    far_row = far_index(ms_row)
    far_col = far_index(ms_col)
    for k in range(DEGREE):
        rows = slice(k * NODES, (k + 1) * NODES)
        r.oh_loc[rows, :] = hot(ms_col[:, k : k + 1] == iota((NODES, NODES), 1))
        r.oh_far[rows, :] = hot(far_col[:, k : k + 1] == iota((NODES, FAR), 1))
    local_rows(0, sender)

    for part in range(2):
        where = iota((NODES, GRID), 0) + part * NODES
        total = jnp.zeros((NODES, GRID), F32)
        for k in range(3):
            total = total + jnp.where(ds_[k : k + 1, :] == where, 1.0, 0.0)
        r.dec_t[part * NODES : (part + 1) * NODES, :] = total.astype(BF)
    r.ns1[...] = mmt(r.dec_t[NODES:, :], r.cp[...]).astype(BF)
    near_start(1, r.ns1, r.nr1)
    r.dext[...] = mmt(r.dec_t[0:NODES, :], r.cp[...])

    def keep(inner, s, value, part, rows):
        r.base[0, rows, :] = inner

    far_rows(0, keep)
    r.mesh[1] = (r.mesh[0].astype(F32) + mm(r.agg[0], wu[0])).astype(BF)

    sender = send_rows(1)
    local_rows(1, sender)

    decode_spread = hot(decode_row == iota((NODES, 4 * HALO), 0))
    near_wait(1, r.ns1, r.nr1)
    decode_back = (r.dext[...] + mm(decode_spread, r.nr1[...])).astype(BF)
    r.dback[...] = decode_back
    latent_back = mm(decode_back, r.dwp[...])
    r.lat[...] = latent_back
    out_back = latent_back.astype(BF)
    r.ob[...] = out_back
    r.ab[...] = mmt(out_back, wu[1])

    def slopes(i, carry):
        rows = pl.ds(pl.multiple_of(i * 64, 64), 64)
        inner = r.base[0, rows, :]
        s = sigmoid(inner)
        r.slope[rows, :] = (s + inner * s * (1.0 - s)).astype(BF)
        return carry

    lax.fori_loop(0, EDGES // 64, slopes, 0)
    for k in range(DEGREE):
        rows = slice(k * NODES, (k + 1) * NODES)
        r.t_loc[:, rows] = hot(ms_row[k : k + 1, :] == iota((NODES, NODES), 0))
        r.t_far[:, rows] = hot(far_row[k : k + 1, :] == iota((FAR, NODES), 0))
    for i in range(SLOTS):
        row = ml[i : i + 1, :]
        r.list_t[:, i * PEERS : (i + 1) * PEERS] = hot(row == iota((NODES, PEERS), 0))

    index = iota((NODES, LATENT), 0)
    named = iota((NODES, LATENT), 1)
    by_band = (index // 64) * 128 + (index % 16) * 8 + (index // 16) % 4
    by_place = (index // 16) * 8 + ((index // 4) % 4) * 128 + index % 4
    for order, first in enumerate((by_band, by_place)):
        r.p_own[order] = hot(first + core * 4 == named)
        r.p_oth[order] = hot(first + (1 - core) * 4 == named)

    r.back[...] = jnp.zeros((NODES, LATENT), F32)

    def turn(inner, s, value, part, rows):
        back = r.ab[part, :] * (s + value * (1.0 - s))
        r.back[part, :] += back
        r.ib[rows, :] = back.astype(BF)

    far_rows(1, turn)
    r.rb[...] = r.back[...].astype(BF)

    def edges_back(i, carry):
        at = pl.multiple_of(i * chunk, chunk)
        back = jnp.zeros((chunk, LATENT), F32)
        given = r.ab[pl.ds(at, chunk), :]
        for k in range(DEGREE):
            rows = pl.ds(k * NODES + at, chunk)
            edge = given * r.slope[rows, :].astype(F32)
            back = back + edge
            r.ib[rows, :] = edge.astype(BF)
        r.rb[pl.ds(at, chunk), :] = back.astype(BF)
        return carry

    def return_start(slot):
        for group in range(2):
            rows = slice(group * (FAR // 2), (group + 1) * (FAR // 2))
            pack(mm(r.t_far[rows, :], r.ib[...]), r.fars[slot].source, group * half)
            far_start(slot, group, True)

    def return_local(layer):
        r.sback[...] = mm(r.t_loc[...], r.ib[...])
        r.lat[...] += mmt(r.rb[...], wr[layer])

    def return_end(slot, layer):
        unpack(r.fars[slot].target)
        sender_b = (r.sback[...] + mm(r.list_t[...], r.far[...])).astype(BF)
        r.lat[...] += mmt(sender_b, ws[layer])
        return sender_b

    return_start(2)
    mesh_last = (r.mesh[1].astype(F32) + mm(r.agg[1], wu[1])).astype(BF)
    r.mesh[2] = mesh_last
    r.mesh_ext[0:NODES, :] = mesh_last
    decode_pick = hot(column(decode_row) == iota((4 * HALO, NODES), 1))
    r.ns2[...] = mm(decode_pick, mesh_last).astype(BF)
    halo_mesh = r.mesh_ext.at[pl.ds(NODES, 4 * HALO)]
    near_start(2, r.ns2, halo_mesh)
    return_local(1)
    gradient(g_u1, 0, r.ob[...], r.agg[1])
    core_start(g_u1)
    gradient(g_r1, 0, r.rb[...], r.mesh[1])
    core_start(g_r1)
    gradient(g_dc, 0, mesh_last, r.dback[...])
    core_start(g_dc)
    for part in range(5):
        where_t = iota((256, NODES), 0) + part * 256
        total_t = jnp.zeros((256, NODES), F32)
        for k in range(DEGREE):
            total_t = total_t + jnp.where(es[k : k + 1, :] == where_t, 1.0, 0.0)
        r.enc_t[part * 256 : (part + 1) * 256, :] = total_t.astype(BF)
    first_start(g_u1)
    first_start(g_r1)
    first_start(g_dc)
    far_wait(2, 0)
    far_wait(2, 1)
    sender_b1 = return_end(2, 1)

    out_back = r.lat[...].astype(BF)
    r.ob[...] = out_back
    r.ab[...] = mmt(out_back, wu[0])
    lax.fori_loop(0, NODES // chunk, edges_back, 0)
    return_start(3)
    return_local(0)
    gradient(g_su, 0, sender_b1, r.mesh[1])
    gradient(g_su, 512, r.ob[...], r.agg[0])
    core_start(g_su)
    gradient(g_r0, 0, r.rb[...], r.mesh[0])
    core_start(g_r0)
    near_wait(2, r.ns2, halo_mesh)
    decoded = mmt(r.dwp[...], r.mesh_ext[...]).astype(BF)
    forecast = r.xp[...].astype(F32) + mm(decoded, r.dec_t[...])
    out_pred[...] = forecast[0:CHANNELS, :].astype(BF)
    first_start(g_su)
    first_start(g_r0)
    second_start(g_u1)
    second_start(g_r1)
    second_start(g_dc)
    far_wait(3, 0)
    far_wait(3, 1)
    sender_b0 = return_end(3, 0)

    encode_back = (r.lat[...] * r.enc_slope[...]).astype(BF)
    input_back = mmt(encode_back, wn[...]).astype(BF)
    r.ns3[...] = mm(r.enc_t[GRID:, :], input_back).astype(BF)
    near_start(3, r.ns3, r.nr3)
    gradient(g_se, 0, sender_b0, r.mesh[0])
    gradient(g_se, 512, encode_back, r.enc_in[...])
    core_start(g_se)
    r.gback[...] = mm(r.enc_t[0:GRID, :], input_back)
    encode_spread = hot(encode_row == iota((GRID, 4 * HALO), 0))
    first_start(g_se)
    second_start(g_su)
    second_start(g_r0)
    near_wait(3, r.ns3, r.nr3)
    r.gback[...] += mm(encode_spread, r.nr3[...])
    r.eb[...] = (r.gback[...] * r.gslope[...].astype(F32)).astype(BF)
    across = mm(r.xp[...], r.eb[...]).astype(BF)
    g_em.sc[...] = mmt(r.p_oth[0], across).astype(BF)
    core_start(g_em)
    g_em.own[...] = mmt(r.p_own[0], across)

    def into(ref, layer=None):
        def write(j, value):
            if layer is None:
                ref[:, j * 128 : (j + 1) * 128] = value
            else:
                ref[layer, :, j * 128 : (j + 1) * 128] = value

        return write

    def deliver_padded(total, ref):
        ref[:, 0:128] = total[0:4, :]
        ref[:, 128:CHANNELS] = total[4:8, 0 : CHANNELS - 128]

    deliver(finish(g_u1), 0, into(out_refresh, 1))
    deliver(finish(g_r1), 0, into(out_target, 1))
    first_start(g_em)
    deliver_padded(finish(g_dc), out_decode)
    total = finish(g_su)
    deliver(total, 0, into(out_source, 1))
    deliver(total, 512, into(out_refresh, 0))
    deliver(finish(g_r0), 0, into(out_target, 0))
    second_start(g_se)
    second_start(g_em)
    total = finish(g_se)
    deliver(total, 0, into(out_source, 0))
    deliver(total, 512, into(out_encode))
    deliver_padded(finish(g_em), out_embed)


def hand_over(*refs):
    for source, target in zip(refs[:7], refs[7:]):
        target[...] = source[...]


def on_device(
    lattice_feature_values,
    cotangent,
    embed_weight,
    encode_weight,
    sender_weight,
    receiver_weight,
    update_weight,
    decode_weight,
    encode_lists,
    encode_sources,
    mesh_lists,
    mesh_sources,
    decode_lists,
    decoder_edge_sources,
):
    spec, tree = jax.tree.flatten(scratch())
    whole = pl.BlockSpec(memory_space=pltpu.VMEM)
    far = pl.BlockSpec(memory_space=pl.ANY)
    shape = jax.ShapeDtypeStruct
    shapes = (
        shape((CHANNELS, GRID), BF),
        shape((4, CHANNELS), F32),
        shape((4, LATENT), F32),
        shape((2, 4, LATENT), F32),
        shape((2, 4, LATENT), F32),
        shape((2, 4, LATENT), F32),
        shape((4, CHANNELS), F32),
    )
    outs = pl.pallas_call(
        functools.partial(kernel, tree),
        out_shape=shapes,
        in_specs=[whole, far, whole, far, far, far, far] + [whole] * 7,
        out_specs=(whole,) * 7,
        scratch_shapes=spec,
        compiler_params=pltpu.CompilerParams(
            collective_id=0, has_side_effects=True, vmem_limit_bytes=60 * 1024 * 1024
        ),
    )(
        lattice_feature_values.T,
        cotangent.T,
        embed_weight,
        encode_weight,
        sender_weight,
        receiver_weight,
        update_weight,
        decode_weight.T,
        encode_lists,
        encode_sources.T,
        mesh_lists.T,
        mesh_sources.T,
        decode_lists,
        decoder_edge_sources.T,
    )
    outs = pl.pallas_call(
        hand_over,
        out_shape=shapes,
        in_specs=[whole] * 7,
        out_specs=(whole,) * 7,
    )(*outs)
    return (
        outs[0].T,
        outs[1].T,
        outs[2].T,
        outs[3].transpose(0, 2, 1),
        outs[4].transpose(0, 2, 1),
        outs[5].transpose(0, 2, 1),
        outs[6],
    )


def solution(mesh):
    return jax.shard_map(
        on_device,
        mesh=mesh,
        in_specs=(
            P(("lat", "lon"), None),
            P(("lat", "lon"), None),
            P(),
            P(),
            P(),
            P(),
            P(),
            P(),
            P(("lat", "lon"), None),
            P(("lat", "lon"), None),
            P(("lat", "lon"), None),
            P(("lat", "lon"), None),
            P(("lat", "lon"), None),
            P(("lat", "lon"), None),
        ),
        out_specs=(
            P(("lat", "lon"), None),
            P(None, ("lat", "lon")),
            P(None, ("lat", "lon")),
            P(None, None, ("lat", "lon")),
            P(None, None, ("lat", "lon")),
            P(None, None, ("lat", "lon")),
            P(("lat", "lon"), None),
        ),
        check_vma=False,
    )
```
